256 devices in a mesh: grp: 16 (over y, x), dev: 16 (over z, core).
Axes of the slice: x: 4, y: 4, z: 8, core: 2. Of those that a mesh axis runs over, the one named last changes fastest.
Arguments:
- old_state: float32 [12288, 5, 2, 512], P(('grp', 'dev')), may hold values from -6 to 6
- old_count: int32 [256], P(('grp', 'dev')), may hold values from 28 to 36, as said below
- new_count: int32 [256], P(('grp', 'dev')), may hold values from 16 to 48, as said below
- column_order: int32 [12288], P(('grp', 'dev')), may hold values from 3 to 7
- neighbour: int32 [4, 12288], P(None, ('grp', 'dev')), may hold values from -1 to 8191, as said below
- face_code: int32 [4, 12288], P(None, ('grp', 'dev')), may hold values from 0 to 7
Outputs:
- new_state: float32 [12288, 5, 2, 512], P(('grp', 'dev'))
The draws below stay inside these ranges and needn't reach their ends.
Inputs may be any that keep to these rules, and one draw needn't show every extreme that they name: `old_count`: migration keeps the curve order; across each boundary between curve-adjacent devices at most 6 columns move, exactly 6 at some boundary; the counts sum to 8192. `new_count`: the counts sum to the same total as old_count; some device holds exactly 48 and some exactly 16. Every neighbour's curve index differs from the column's own by at most 16; slots beyond new_count have -1.
All inputs are finite; a program needn't handle non-finite values.
Results may differ from the reference program's by a relative error of at most 0.0003.
Values sent between devices are 32-bit elements; how exact they have to be, the bound alone decides.
No kernel may reach another device: no remote copies, remote signals or barrier semaphores. Data moves between devices by JAX's collectives and lax.ppermute only.
A program may use at most 64 MiB of HBM per device.

```python
import jax
import jax.numpy as jnp
import numpy as np
from jax import lax

CAP = 48
LEV = 2
MODES = 8
VARS = 5
MOVE = 6
ROW = 8
SHARDS = 256
COLS = 12288


def plan_counts(key):
    subkeys = jax.random.split(key, 4)
    middle = CAP * 2 // 3
    spread = CAP // 12
    half = SHARDS // 2
    busiest = jax.random.randint(subkeys[2], (), 3, half - 1)
    offsets = jax.random.randint(subkeys[0], (half,), -spread, spread + 1)
    offsets = jnp.where(jnp.arange(half) == busiest, spread, offsets)
    old_count = jnp.concatenate([middle + offsets, middle - offsets])
    lightest = busiest + half
    shifts = jax.random.randint(subkeys[1], (SHARDS + 1,), -MOVE, MOVE + 1)
    bounds = jnp.arange(SHARDS + 1)
    shifts = jnp.where(bounds == 1, -MOVE, shifts)
    shifts = jnp.where(bounds == 2, MOVE, shifts)
    shifts = jnp.where(bounds == busiest, -MOVE, shifts)
    shifts = jnp.where(bounds == busiest + 1, MOVE, shifts)
    shifts = jnp.where(bounds == lightest, MOVE, shifts)
    shifts = jnp.where(bounds == lightest + 1, -MOVE, shifts)
    shifts = jnp.where((bounds == 0) | (bounds == SHARDS), 0, shifts)
    new_count = old_count + shifts[1:] - shifts[:-1]
    lowest = CAP * 7 // 12
    panel_row = jax.random.randint(subkeys[3], (), 1, SHARDS * lowest // ROW)
    return (old_count.astype(jnp.int32), new_count.astype(jnp.int32), panel_row)


def column_geometry(key):
    old_count, new_count, panel_row = plan_counts(key)
    total = jnp.sum(new_count)
    starts = jnp.cumsum(new_count) - new_count
    column = jnp.arange(SHARDS * CAP)
    owner = column // CAP
    within = column % CAP
    curve = starts[owner] + within
    valid = within < new_count[owner]
    row_of = curve // ROW
    offset = curve % ROW
    across = jnp.where(row_of % 2 == 0, offset, ROW - 1 - offset)
    second = row_of >= panel_row
    step_sign = jnp.where(second, -1, 1)
    target_row = jnp.stack([row_of, row_of, row_of - step_sign, row_of + step_sign])
    target_col = jnp.stack([across - step_sign, across + step_sign, across, across])
    target = target_row * ROW + jnp.where(target_row % 2 == 0, target_col, ROW - 1 - target_col)
    inside = (target_col >= 0) & (target_col < ROW) & (target_row >= 0) & valid[None, :] & (target < total)
    same_panel = (target_row >= panel_row) == second[None, :]
    faces = jnp.arange(4)[:, None] * jnp.ones_like(target)
    facing = jnp.where(same_panel, jnp.bitwise_xor(faces, 1), faces)
    flipped = jnp.where(same_panel, 0, 1)
    neighbour = jnp.where(inside, target, -1)
    face_code = jnp.where(inside, 2 * facing + flipped, 0)
    return (neighbour.astype(jnp.int32), face_code.astype(jnp.int32))


def draw_old_count(key, part):
    return plan_counts(key)[0]


def draw_new_count(key, part):
    return plan_counts(key)[1]


def draw_neighbour(key, part):
    return column_geometry(key)[0]


def draw_face_code(key, part):
    return column_geometry(key)[1]


def plant(drawn, key, least, high):
    dims = drawn.shape
    spot = [jax.random.randint(jax.random.fold_in(key, axis), (), 0, dims[axis]) for axis in range(len(dims))]
    drawn = drawn.at[tuple(spot)].set(least)
    longest = dims.index(max(dims))
    spot[longest] = (spot[longest] + 1) % dims[longest]
    return drawn.at[tuple(spot)].set(high)


def level_of(key, dims, cuts, low, largest):
    gain, own = 1.0, jax.random.fold_in(key, 6)
    for axis_at, parts in cuts:
        heights = jnp.exp(jax.random.uniform(jax.random.fold_in(own, axis_at), (parts,), jnp.float32, low / len(cuts), largest / len(cuts)))
        gain = gain * jnp.repeat(heights, dims[axis_at] // parts).reshape([-1 if axis == axis_at else 1 for axis in range(len(dims))])
    return gain


def normal_values(stream_key, shape, scale, limit, cuts=(), kind=jnp.bfloat16):
    entries = jax.random.normal(stream_key, shape, jnp.float32) * scale
    if len(cuts) > 0:
        entries = level_of(stream_key, shape, cuts, -0.22, 0.18) * entries
    return jnp.clip(entries, min=-limit, max=limit).astype(kind)


def setup_inputs(seed: int = 0) -> dict:
    key_of = jax.random.split(jax.random.key(seed), 7)
    return {
        "old_state": normal_values(key_of[0], (COLS, VARS, LEV, MODES * MODES * MODES), 1.0, 6.0, ((0, 256),), jnp.float32),
        "old_count": draw_old_count(jax.random.fold_in(key_of[6], 71), 0),
        "new_count": draw_new_count(jax.random.fold_in(key_of[6], 71), 0),
        "column_order": plant(jax.random.randint(key_of[3], (COLS,), 3, 8), jax.random.fold_in(key_of[3], 1), 3, 7).astype(jnp.int32),
        "neighbour": draw_neighbour(jax.random.fold_in(key_of[6], 71), 0),
        "face_code": draw_face_code(jax.random.fold_in(key_of[6], 71), 0),
    }


HIGHEST_PRECISION = lax.Precision.HIGHEST
HORIZ_SCALE = 2.0
VERT_SCALE = 4.0
TIME_STEP = 0.005
BUOYANCY = 1.0

def mode_tables():
    degree = np.arange(8)
    edge_plus = np.sqrt((2.0 * degree + 1.0) / 2.0)
    edge_minus = edge_plus * (-1.0) ** degree
    derivative = np.zeros((8, 8))
    for low_mode in range(8):
        for high_mode in range(low_mode + 1, 8, 2):
            derivative[low_mode, high_mode] = np.sqrt((2.0 * low_mode + 1.0) * (2.0 * high_mode + 1.0))
    parity = (-1.0) ** degree
    return (jnp.asarray(edge_plus, jnp.float32), jnp.asarray(edge_minus, jnp.float32), jnp.asarray(derivative, jnp.float32), jnp.asarray(parity, jnp.float32))

def order_mask(column_order):
    modes = jnp.arange(512, dtype=jnp.int32)
    highest = jnp.maximum(jnp.maximum(modes // 64, modes // 8 % 8), modes % 8)
    return (highest[None, :] <= column_order[:, None]).astype(jnp.float32)

def across_x(field, edge):
    return jnp.einsum('k,nlzky->nlzy', edge, field, precision=HIGHEST_PRECISION)

def across_y(field, edge):
    return jnp.einsum('k,nlzxk->nlzx', edge, field, precision=HIGHEST_PRECISION)

def across_z(field, edge):
    return jnp.einsum('k,nlkxy->nlxy', edge, field, precision=HIGHEST_PRECISION)

def face_traces(coeffs):
    edge_plus, edge_minus, derivative, parity = mode_tables()
    count = coeffs.shape[0]
    levels = coeffs.shape[2]
    cube = coeffs.reshape(count, 5, levels, 8, 8, 8)
    pressure = cube[:, 0]
    velo_x = cube[:, 1]
    velo_y = cube[:, 2]
    faces_mass = jnp.stack([across_x(pressure, edge_minus), across_x(pressure, edge_plus), across_y(pressure, edge_minus), across_y(pressure, edge_plus)], axis=1)
    faces_flow = jnp.stack([-across_x(velo_x, edge_minus), across_x(velo_x, edge_plus), -across_y(velo_y, edge_minus), across_y(velo_y, edge_plus)], axis=1)
    return jnp.stack([faces_mass, faces_flow], axis=2).reshape(count, 4, 2, levels * 64)

def tendency(coeffs, inside, outside, wall, flipped):
    edge_plus, edge_minus, derivative, parity = mode_tables()
    count = coeffs.shape[0]
    levels = coeffs.shape[2]
    cube = coeffs.reshape(count, 5, levels, 8, 8, 8)
    pressure, velo_x, velo_y, velo_z, buoyancy = (cube[:, 0], cube[:, 1], cube[:, 2], cube[:, 3], cube[:, 4])

    def along_x(field):
        return jnp.einsum('jk,nlzky->nlzjy', derivative, field, precision=HIGHEST_PRECISION)

    def along_y(field):
        return jnp.einsum('jk,nlzxk->nlzxj', derivative, field, precision=HIGHEST_PRECISION)

    def along_z(field):
        return jnp.einsum('jk,nlkxy->nljxy', derivative, field, precision=HIGHEST_PRECISION)

    def lift_x(jump, edge):
        return edge[:, None] * jump[:, :, :, None, :]

    def lift_y(jump, edge):
        return jump[..., None] * edge

    def lift_z(jump, edge):
        return edge[:, None, None] * jump[:, :, None]
    inner = inside.reshape(count, 4, 2, levels, 8, 8)
    outer = outside.reshape(count, 4, 2, levels, 8, 8)
    turned = 1.0 + flipped[:, :, None, None, None] * (parity - 1.0)
    facing_wall = wall[:, :, None, None, None]
    inner_mass = inner[:, :, 0]
    inner_flow = inner[:, :, 1]
    outer_mass = jnp.where(facing_wall, inner_mass, outer[:, :, 0] * turned)
    outer_flow = jnp.where(facing_wall, -inner_flow, -outer[:, :, 1] * turned)
    jump_mass = 0.5 * (inner_flow - outer_flow) + 0.5 * (outer_mass - inner_mass)
    jump_flow = 0.5 * (inner_mass - outer_mass) + 0.5 * (outer_flow - inner_flow)
    top_mass = across_z(pressure, edge_plus)
    bottom_mass = across_z(pressure, edge_minus)
    top_flow = across_z(velo_z, edge_plus)
    bottom_flow = across_z(velo_z, edge_minus)
    above_mass = jnp.concatenate([bottom_mass[:, 1:], top_mass[:, -1:]], axis=1)
    above_flow = jnp.concatenate([bottom_flow[:, 1:], -top_flow[:, -1:]], axis=1)
    below_mass = jnp.concatenate([bottom_mass[:, :1], top_mass[:, :-1]], axis=1)
    below_flow = jnp.concatenate([bottom_flow[:, :1], -top_flow[:, :-1]], axis=1)
    top_jump_mass = 0.5 * (top_flow - above_flow) + 0.5 * (above_mass - top_mass)
    top_jump_flow = 0.5 * (top_mass - above_mass) + 0.5 * (above_flow - top_flow)
    bottom_inner = -bottom_flow
    bottom_jump_mass = 0.5 * (bottom_inner - below_flow) + 0.5 * (below_mass - bottom_mass)
    bottom_jump_flow = 0.5 * (bottom_mass - below_mass) + 0.5 * (below_flow - bottom_inner)
    rate_mass = -HORIZ_SCALE * (along_x(velo_x) + along_y(velo_y)) - VERT_SCALE * along_z(velo_z) + HORIZ_SCALE * (lift_x(jump_mass[:, 0], edge_minus) + lift_x(jump_mass[:, 1], edge_plus) + lift_y(jump_mass[:, 2], edge_minus) + lift_y(jump_mass[:, 3], edge_plus)) + VERT_SCALE * (lift_z(top_jump_mass, edge_plus) + lift_z(bottom_jump_mass, edge_minus))
    rate_x = -HORIZ_SCALE * along_x(pressure) + HORIZ_SCALE * (lift_x(jump_flow[:, 1], edge_plus) - lift_x(jump_flow[:, 0], edge_minus))
    rate_y = -HORIZ_SCALE * along_y(pressure) + HORIZ_SCALE * (lift_y(jump_flow[:, 3], edge_plus) - lift_y(jump_flow[:, 2], edge_minus))
    rate_z = -VERT_SCALE * along_z(pressure) + buoyancy + VERT_SCALE * (lift_z(top_jump_flow, edge_plus) - lift_z(bottom_jump_flow, edge_minus))
    rate_buoy = -BUOYANCY * velo_z
    return jnp.stack([rate_mass, rate_x, rate_y, rate_z, rate_buoy], axis=1).reshape(count, 5, levels, 512)

def owner_slot(curve, begin, capacity):
    owner = lax.optimization_barrier(jnp.sum((begin[None, :] <= curve[:, None]).astype(jnp.int32), axis=1)).astype(jnp.int32) - 1
    owner = jnp.maximum(owner, 0)
    return (owner * capacity + curve - begin[owner]).astype(jnp.int32)

def reference(old_state, old_count, new_count, column_order, neighbour, face_code):
    shards = old_count.shape[0]
    capacity = old_state.shape[0] // shards
    levels = old_state.shape[2]
    old_begin = (jnp.cumsum(old_count) - old_count).astype(jnp.int32)
    new_begin = (jnp.cumsum(new_count) - new_count).astype(jnp.int32)
    column = jnp.arange(shards * capacity, dtype=jnp.int32)
    owner = column // capacity
    within = column % capacity
    curve = new_begin[owner] + within
    valid = within < new_count[owner]
    source = jnp.where(valid, owner_slot(curve, old_begin, capacity), 0)
    mask = order_mask(column_order) * valid[:, None].astype(jnp.float32)
    start_state = old_state[source] * mask[:, None, None, :]
    target = neighbour.T
    wall = target < 0
    target_slot = owner_slot(target.reshape(-1), new_begin, capacity).reshape(target.shape)
    target_slot = jnp.where(wall, 0, target_slot)
    row_pick = (target_slot * 4 + face_code.T // 2).reshape(-1).astype(jnp.int32)
    flipped = (face_code.T % 2).astype(jnp.float32)
    width = levels * 64

    def evaluate(coeffs):
        blocks = coeffs.reshape(shards, capacity, 5, levels, 512)
        traces = lax.map(face_traces, blocks)
        flat = traces.reshape(-1, 2, width)
        outside = jnp.take(flat, row_pick, axis=0).reshape(shards, capacity, 4, 2, width)

        def one_block(pieces):
            return tendency(pieces[0], pieces[1], pieces[2], pieces[3], pieces[4])
        rates = lax.map(one_block, (blocks, traces, outside, wall.reshape(shards, capacity, 4), flipped.reshape(shards, capacity, 4)))
        return rates.reshape(coeffs.shape) * mask[:, None, None, :]
    first = start_state + TIME_STEP * evaluate(start_state)
    return 0.5 * start_state + 0.5 * (first + TIME_STEP * evaluate(first))
```

```python
import jax
import jax.numpy as jnp
import numpy as np
from jax import lax
from jax.experimental import pallas as pl
from jax.experimental.pallas import tpu as pltpu
from jax.sharding import PartitionSpec as P

TIME_STEP = 0.005
CAP = 48
ROWS = 40
REACH = 32
FAR = 10
MARGIN = 24
LANES = 128
SCALE = [float(np.sqrt(2.0 * k + 1.0)) for k in range(8)]


def fetch(win, sems, own, left, right, far_left, far_right, shift, own_count, left_count, right_count):
    def copy(source, first, count, lane, which):
        source_rows = pl.ds(pl.multiple_of(first * ROWS, 8), count * ROWS)
        target_rows = pl.ds(pl.multiple_of((lane + MARGIN) * ROWS, 8), count * ROWS)
        return pltpu.make_async_copy(source.at[source_rows], win.at[target_rows], sems.at[which])

    return [
        copy(own, 0, own_count, shift, 0),
        copy(left, 0, left_count, shift - left_count, 1),
        copy(right, 0, right_count, shift + own_count, 2),
        copy(far_left, 0, FAR, shift - left_count - FAR, 3),
        copy(far_right, 0, FAR, shift + own_count + right_count, 4),
    ]


def traces(state, lev, rise, fall):
    for z in range(8):
        along = [(0, 1), (2, 3)]
        for direction in range(2):
            sums = []
            for field in (0, 1 + direction):
                even = odd = None
                for k in range(8):
                    if direction == 0 or field == 2:
                        part = state[field, lev, pl.ds(z * 64 + k * 8, 8), :]
                    else:
                        part = state[field, lev, pl.ds(z * 64 + k, 8, stride=8), :]
                    if k == 0:
                        even = part
                    elif k == 1:
                        odd = part
                    elif k % 2 == 0:
                        even = even + part
                    else:
                        odd = odd + part
                sums.append((even - odd, even + odd))
            (mass_low, mass_high), (flow_low, flow_high) = sums
            low, high = along[direction]
            spot = pl.ds(z * 8, 8)
            rise[low, lev, spot, :] = mass_low - flow_low
            fall[low, lev, spot, :] = -flow_low - mass_low
            rise[high, lev, spot, :] = mass_high + flow_high
            fall[high, lev, spot, :] = flow_high - mass_high


def upright(state, lift):
    for x in range(8):
        ends = []
        for lev in range(2):
            sums = []
            for field in (0, 3):
                even = odd = None
                for z in range(8):
                    part = state[field, lev, pl.ds(z * 64 + x * 8, 8), :]
                    if z == 0:
                        even = part
                    elif z == 1:
                        odd = part
                    elif z % 2 == 0:
                        even = even + part
                    else:
                        odd = odd + part
                sums.append((even - odd, even + odd))
            ends.append(sums)
        ((mass_b0, mass_t0), (flow_b0, flow_t0)), ((mass_b1, mass_t1), (flow_b1, flow_t1)) = ends
        bottom0 = -2.0 * flow_b0
        top0 = (flow_t0 - mass_t0) + (mass_b1 - flow_b1)
        bottom1 = (mass_t0 + flow_t0) - (flow_b1 + mass_b1)
        top1 = 2.0 * flow_t1
        spot = pl.ds(x * 8, 8)
        lift[0, 0, spot, :] = 0.25 * (top0 + bottom0)
        lift[0, 1, spot, :] = 0.25 * (top0 - bottom0)
        lift[1, 0, spot, :] = 0.25 * (top1 + bottom1)
        lift[1, 1, spot, :] = 0.25 * (top1 - bottom1)


def jumps(lev, rise, fall, lanes, sources, signs, z):
    spot = pl.ds(z * 8, 8)
    parts = [rise[source, lev, spot, :] for source in range(4)]
    whole = []
    for face in range(4):
        picked = [
            jnp.take_along_axis(part, lanes[face], axis=1, mode="promise_in_bounds") for part in parts
        ]
        lower = jnp.where(sources[face] == 0, picked[0], picked[1])
        upper = jnp.where(sources[face] == 2, picked[2], picked[3])
        outer = jnp.where(sources[face] < 2, lower, upper)
        whole.append(fall[face, lev, spot, :] + signs[face] * outer)
    west, east, south, north = whole
    return (
        0.25 * (east + west),
        0.25 * (east - west),
        0.25 * (north + south),
        0.25 * (north - south),
    )


def section(state, base, result, rise, fall, lift, side, masks, lanes, sources, signs, last):
    step = TIME_STEP

    def put(field, lev, spot, old, change, mask):
        fresh = old + mask * change
        if last:
            fresh = 0.5 * base[field, lev, spot, :] + 0.5 * fresh
        result[field, lev, spot, :] = fresh

    upright(state, lift)

    @pl.loop(0, 2)
    def _(lev):
        traces(state, lev, rise, fall)
        tops = [[lift[lev, part, pl.ds(x * 8, 8), :] for x in range(8)] for part in range(2)]
        up_mass = [[tops[0][x], tops[1][x]] for x in range(8)]
        up_flow = [[-tops[1][x], -tops[0][x]] for x in range(8)]
        for z in reversed(range(8)):
            sum_x, diff_x, sum_y, diff_y = jumps(lev, rise, fall, lanes, sources, signs, z)
            mass = [sum_y, diff_y]
            flow = [-diff_y, -sum_y]
            for y in reversed(range(8)):
                spot = pl.ds(z * 64 + y * 8, 8)
                turned = pl.ds(z * 64 + y, 8, stride=8)
                parity = y % 2
                side[turned, :] = (step * 2.0 * (2 * y + 1)) * mass[parity]
                here_flow = state[2, lev, spot, :]
                put(2, lev, spot, here_flow, (step * 2.0 * (2 * y + 1)) * flow[parity], masks[max(z, y)])
                if y > 0:
                    mass[1 - parity] = mass[1 - parity] - here_flow
                    flow[1 - parity] = flow[1 - parity] - state[0, lev, turned, :]
            mass = [sum_x, diff_x]
            flow = [-diff_x, -sum_x]
            for x in reversed(range(8)):
                spot = pl.ds(z * 64 + x * 8, 8)
                parity, upright_parity = x % 2, z % 2
                mask = masks[max(z, x)]
                here_mass = state[0, lev, spot, :]
                here_flow = state[1, lev, spot, :]
                here_up = state[3, lev, spot, :]
                here_lift = state[4, lev, spot, :]
                change = (
                    (step * 2.0 * (2 * x + 1)) * mass[parity]
                    + (step * 4.0 * (2 * z + 1)) * up_mass[x][upright_parity]
                    + side[spot, :]
                )
                put(0, lev, spot, here_mass, change, mask)
                put(1, lev, spot, here_flow, (step * 2.0 * (2 * x + 1)) * flow[parity], mask)
                change = (step * 4.0 * (2 * z + 1)) * up_flow[x][upright_parity] + step * here_lift
                put(3, lev, spot, here_up, change, mask)
                put(4, lev, spot, here_lift, -step * here_up, mask)
                if x > 0:
                    mass[1 - parity] = mass[1 - parity] - here_flow
                    flow[1 - parity] = flow[1 - parity] - here_mass
                if z > 0:
                    other = 1 - upright_parity
                    up_mass[x][other] = up_mass[x][other] - here_up
                    up_flow[x][other] = up_flow[x][other] - here_mass


def body(
    begins,
    place,
    table,
    table_left,
    table_right,
    near,
    near_left,
    near_right,
    order_left,
    order_right,
    own,
    left,
    right,
    far_left,
    far_right,
    out,
    win,
    start,
    first,
    rise,
    fall,
    lift,
    side,
    sems,
):
    dev = place[0]
    old_begin = begins[0, dev]
    new_begin = begins[1, dev]
    own_count, own_new = table[0], table[1]
    left_count, left_new = table_left[0], table_left[1]
    right_count, right_new = table_right[0], table_right[1]
    shift = REACH + old_begin - new_begin
    copies = fetch(
        win, sems, own, left, right, far_left, far_right, shift, own_count, left_count, right_count
    )
    for copy in copies:
        copy.start()
    lane = lax.broadcasted_iota(jnp.int32, (16, LANES), 1)
    after = REACH + own_new
    before = REACH - left_new

    def turn(values, amount):
        return pltpu.roll(values, jnp.bitwise_and(amount, LANES - 1), 1)

    window = jnp.where(
        lane < REACH,
        turn(near_left[...], before),
        jnp.where(lane < after, turn(near[...], REACH), turn(near_right[...], after)),
    )
    order = window[8:16, :][0:1, :]
    far_before = turn(order_left[...], before - 16)[0:1, :].astype(jnp.int32)
    far_after = turn(order_right[...], after + right_new)[0:1, :].astype(jnp.int32)
    row_lane = lax.broadcasted_iota(jnp.int32, (1, LANES), 1)
    order = jnp.where(row_lane < before, far_before, order)
    order = jnp.where(row_lane >= after + right_new, far_after, order)
    order = jnp.broadcast_to(order, (8, LANES))
    minor = lax.broadcasted_iota(jnp.int32, (8, LANES), 0)
    lane8 = lax.broadcasted_iota(jnp.int32, (8, LANES), 1)
    masks = [(jnp.maximum(minor, n) <= order).astype(jnp.float32) for n in range(8)]
    root = jnp.sqrt((2 * minor + 1).astype(jnp.float32))
    lanes, sources, signs = [], [], []
    for face in range(4):
        target = jnp.broadcast_to(window[face : face + 1, :], (8, LANES))
        code = jnp.broadcast_to(window[4 + face : 5 + face, :], (8, LANES))
        wall = target < 0
        lanes.append(jnp.bitwise_and(jnp.where(wall, lane8, target - new_begin + REACH), LANES - 1))
        sources.append(jnp.where(wall, face, code >> 1))
        odd = jnp.bitwise_and(code, 1) * jnp.bitwise_and(minor, 1)
        signs.append(jnp.where(wall, 1.0, 1.0 - 2.0 * odd.astype(jnp.float32)))
    for copy in copies:
        copy.wait()
    scaled = [masks[n] * root for n in range(8)]

    @pl.loop(0, 2)
    def _(lev):
        for field in range(5):
            for part in range(4):
                block = win[pl.ds(MARGIN * ROWS + field * 8 + part * 2 + lev, LANES, stride=ROWS), :].T
                for z in (2 * part, 2 * part + 1):
                    for x in range(8):
                        at = (z - 2 * part) * 64 + x * 8
                        value = block[at : at + 8, :] * scaled[max(z, x)] * (SCALE[z] * SCALE[x])
                        if field == 2:
                            start[field, lev, pl.ds(z * 64 + x, 8, stride=8), :] = value
                        else:
                            start[field, lev, pl.ds(z * 64 + x * 8, 8), :] = value

    section(start, None, first, rise, fall, lift, side, masks, lanes, sources, signs, False)
    section(first, start, start, rise, fall, lift, side, masks, lanes, sources, signs, True)
    valid = jnp.logical_and(lane8 >= REACH, lane8 < after)
    shrink = jnp.where(valid, 1.0 / root, 0.0)

    @pl.loop(0, 2)
    def _(lev):
        for field in range(5):
            for part in range(4):
                pieces = []
                for z in (2 * part, 2 * part + 1):
                    for x in range(8):
                        if field == 2:
                            value = start[field, lev, pl.ds(z * 64 + x, 8, stride=8), :]
                        else:
                            value = start[field, lev, pl.ds(z * 64 + x * 8, 8), :]
                        value = value * shrink * (1.0 / (SCALE[z] * SCALE[x]))
                        pieces.append(jnp.where(valid, value, 0.0))
                block = jnp.concatenate(pieces, axis=0).T
                out[pl.ds(field * 8 + part * 2 + lev, CAP, stride=ROWS), :] = block[REACH : REACH + CAP, :]


def advance(*operands):
    smem = pl.BlockSpec(memory_space=pltpu.SMEM)
    vmem = pl.BlockSpec(memory_space=pltpu.VMEM)
    hbm = pl.BlockSpec(memory_space=pl.ANY)
    return pl.pallas_call(
        body,
        out_shape=jax.ShapeDtypeStruct((CAP * ROWS, LANES), jnp.float32),
        in_specs=[smem] * 5 + [vmem] * 5 + [hbm] * 5,
        out_specs=vmem,
        scratch_shapes=[
            pltpu.VMEM(((MARGIN + LANES) * ROWS, LANES), jnp.float32),
            pltpu.VMEM((5, 2, 512, LANES), jnp.float32),
            pltpu.VMEM((5, 2, 512, LANES), jnp.float32),
            pltpu.VMEM((4, 2, 64, LANES), jnp.float32),
            pltpu.VMEM((4, 2, 64, LANES), jnp.float32),
            pltpu.VMEM((2, 2, 64, LANES), jnp.float32),
            pltpu.VMEM((512, LANES), jnp.float32),
            pltpu.SemaphoreType.DMA((5,)),
        ],
        compiler_params=pltpu.CompilerParams(vmem_limit_bytes=32 * 1024 * 1024),
        name="advance",
    )(*operands)


def local(old_state, old_count, new_count, column_order, neighbour, face_code):
    axes = ("grp", "dev")
    groups, members = lax.axis_size("grp"), lax.axis_size("dev")
    shards = groups * members
    group, member = lax.axis_index("grp"), lax.axis_index("dev")

    def along(values, hop):
        return lax.ppermute(values, axes, [(i, (i + hop) % shards) for i in range(shards)])

    own = old_state.reshape(CAP, 5, 2, 4, LANES).transpose(0, 1, 3, 2, 4).reshape(CAP * ROWS, LANES)
    near = jnp.concatenate([neighbour, face_code, column_order[None, :]], axis=0)
    near = jnp.pad(near, ((0, 7), (0, LANES - CAP)))
    counts = jnp.concatenate([old_count, new_count])

    tail = lax.dynamic_slice_in_dim(own, (old_count[0] - FAR) * ROWS, FAR * ROWS, 0)
    head = own[: FAR * ROWS]
    tail_order = lax.dynamic_slice_in_dim(column_order, new_count[0] - 16, 16, 0)

    def pack(columns, order):
        row = jnp.pad(order.astype(jnp.float32)[None, :], ((0, 7), (0, LANES - order.shape[0])))
        return jnp.concatenate([columns, row], axis=0)

    left, right = along(own, 1), along(own, -1)
    near_left, near_right = along(near, 1), along(near, -1)
    table_left, table_right = along(counts, 1), along(counts, -1)
    far_left, far_right = along(pack(tail, tail_order), 2), along(pack(head, column_order), -2)

    reached = lax.all_to_all(jnp.broadcast_to(counts, (groups, 2)), "grp", 0, 0, tiled=True)
    earlier = jnp.sum(jnp.where(jnp.arange(groups)[:, None] < group, reached, 0), axis=0)
    share = earlier[:, None] + jnp.where(jnp.arange(members)[None, :] > member, counts[:, None], 0)
    begins = lax.psum(share, "dev")
    place = jnp.reshape(member, (1,)).astype(jnp.int32)
    out = advance(
        begins,
        place,
        counts,
        table_left,
        table_right,
        near,
        near_left,
        near_right,
        far_left[FAR * ROWS :],
        far_right[FAR * ROWS :],
        own,
        left,
        right,
        far_left,
        far_right,
    )
    out = out.reshape(CAP, 5, 4, 2, LANES).transpose(0, 1, 3, 2, 4)
    return out.reshape(CAP, 5, 2, 512)


def solution(mesh):
    in_specs = (
        P(("grp", "dev"), None, None, None),
        P(("grp", "dev")),
        P(("grp", "dev")),
        P(("grp", "dev")),
        P(None, ("grp", "dev")),
        P(None, ("grp", "dev")),
    )
    out_specs = P(("grp", "dev"), None, None, None)
    return jax.shard_map(local, mesh=mesh, in_specs=in_specs, out_specs=out_specs, check_vma=False)
```

```python
import jax
import jax.numpy as jnp
import numpy as np
from jax import lax
from jax.experimental import pallas as pl
from jax.experimental.pallas import tpu as pltpu
from jax.sharding import PartitionSpec as P

TIME_STEP = 0.005
CAP = 48
ROWS = 40
REACH = 32
FAR = 10
HELD = 36
MARGIN = 24
LANES = 128
SCALE = [float(np.sqrt(2.0 * k + 1.0)) for k in range(8)]


def fetch(win, sems, own, left, right, far_left, far_right, shift, own_count, left_count, right_count):
    def copy(source, first, count, lane, which):
        source_rows = pl.ds(pl.multiple_of(first * ROWS, 8), count * ROWS)
        target_rows = pl.ds(pl.multiple_of((lane + MARGIN) * ROWS, 8), count * ROWS)
        return pltpu.make_async_copy(source.at[source_rows], win.at[target_rows], sems.at[which])

    return [
        copy(own, 0, own_count, shift, 0),
        copy(left, 0, left_count, shift - left_count, 1),
        copy(right, 0, right_count, shift + own_count, 2),
        copy(far_left, 0, FAR, shift - left_count - FAR, 3),
        copy(far_right, 0, FAR, shift + own_count + right_count, 4),
    ]


def traces(state, lev, rise, fall):
    for z in range(8):
        along = [(0, 1), (2, 3)]
        for direction in range(2):
            sums = []
            for field in (0, 1 + direction):
                even = odd = None
                for k in range(8):
                    if direction == 0 or field == 2:
                        part = state[field, lev, pl.ds(z * 64 + k * 8, 8), :]
                    else:
                        part = state[field, lev, pl.ds(z * 64 + k, 8, stride=8), :]
                    if k == 0:
                        even = part
                    elif k == 1:
                        odd = part
                    elif k % 2 == 0:
                        even = even + part
                    else:
                        odd = odd + part
                sums.append((even - odd, even + odd))
            (mass_low, mass_high), (flow_low, flow_high) = sums
            low, high = along[direction]
            spot = pl.ds(z * 8, 8)
            rise[low, lev, spot, :] = mass_low - flow_low
            fall[low, lev, spot, :] = -flow_low - mass_low
            rise[high, lev, spot, :] = mass_high + flow_high
            fall[high, lev, spot, :] = flow_high - mass_high


def upright(state, lift):
    for x in range(8):
        ends = []
        for lev in range(2):
            sums = []
            for field in (0, 3):
                even = odd = None
                for z in range(8):
                    part = state[field, lev, pl.ds(z * 64 + x * 8, 8), :]
                    if z == 0:
                        even = part
                    elif z == 1:
                        odd = part
                    elif z % 2 == 0:
                        even = even + part
                    else:
                        odd = odd + part
                sums.append((even - odd, even + odd))
            ends.append(sums)
        ((mass_b0, mass_t0), (flow_b0, flow_t0)), ((mass_b1, mass_t1), (flow_b1, flow_t1)) = ends
        bottom0 = -2.0 * flow_b0
        top0 = (flow_t0 - mass_t0) + (mass_b1 - flow_b1)
        bottom1 = (mass_t0 + flow_t0) - (flow_b1 + mass_b1)
        top1 = 2.0 * flow_t1
        spot = pl.ds(x * 8, 8)
        lift[0, 0, spot, :] = 0.25 * (top0 + bottom0)
        lift[0, 1, spot, :] = 0.25 * (top0 - bottom0)
        lift[1, 0, spot, :] = 0.25 * (top1 + bottom1)
        lift[1, 1, spot, :] = 0.25 * (top1 - bottom1)


def jumps(lev, rise, fall, lanes, sources, signs, z):
    spot = pl.ds(z * 8, 8)
    parts = [rise[source, lev, spot, :] for source in range(4)]
    whole = []
    for face in range(4):
        picked = [
            jnp.take_along_axis(part, lanes[face], axis=1, mode="promise_in_bounds") for part in parts
        ]
        lower = jnp.where(sources[face] == 0, picked[0], picked[1])
        upper = jnp.where(sources[face] == 2, picked[2], picked[3])
        outer = jnp.where(sources[face] < 2, lower, upper)
        whole.append(fall[face, lev, spot, :] + signs[face] * outer)
    west, east, south, north = whole
    return (
        0.25 * (east + west),
        0.25 * (east - west),
        0.25 * (north + south),
        0.25 * (north - south),
    )


def section(state, base, result, rise, fall, lift, side, masks, lanes, sources, signs, last):
    step = TIME_STEP

    def put(field, lev, spot, old, change, mask):
        fresh = old + mask * change
        if last:
            fresh = 0.5 * base[field, lev, spot, :] + 0.5 * fresh
        result[field, lev, spot, :] = fresh

    upright(state, lift)

    @pl.loop(0, 2)
    def _(lev):
        traces(state, lev, rise, fall)
        tops = [[lift[lev, part, pl.ds(x * 8, 8), :] for x in range(8)] for part in range(2)]
        up_mass = [[tops[0][x], tops[1][x]] for x in range(8)]
        up_flow = [[-tops[1][x], -tops[0][x]] for x in range(8)]
        for z in reversed(range(8)):
            sum_x, diff_x, sum_y, diff_y = jumps(lev, rise, fall, lanes, sources, signs, z)
            mass = [sum_y, diff_y]
            flow = [-diff_y, -sum_y]
            for y in reversed(range(8)):
                spot = pl.ds(z * 64 + y * 8, 8)
                turned = pl.ds(z * 64 + y, 8, stride=8)
                parity = y % 2
                side[turned, :] = (step * 2.0 * (2 * y + 1)) * mass[parity]
                here_flow = state[2, lev, spot, :]
                put(2, lev, spot, here_flow, (step * 2.0 * (2 * y + 1)) * flow[parity], masks[max(z, y)])
                if y > 0:
                    mass[1 - parity] = mass[1 - parity] - here_flow
                    flow[1 - parity] = flow[1 - parity] - state[0, lev, turned, :]
            mass = [sum_x, diff_x]
            flow = [-diff_x, -sum_x]
            for x in reversed(range(8)):
                spot = pl.ds(z * 64 + x * 8, 8)
                parity, upright_parity = x % 2, z % 2
                mask = masks[max(z, x)]
                here_mass = state[0, lev, spot, :]
                here_flow = state[1, lev, spot, :]
                here_up = state[3, lev, spot, :]
                here_lift = state[4, lev, spot, :]
                change = (
                    (step * 2.0 * (2 * x + 1)) * mass[parity]
                    + (step * 4.0 * (2 * z + 1)) * up_mass[x][upright_parity]
                    + side[spot, :]
                )
                put(0, lev, spot, here_mass, change, mask)
                put(1, lev, spot, here_flow, (step * 2.0 * (2 * x + 1)) * flow[parity], mask)
                change = (step * 4.0 * (2 * z + 1)) * up_flow[x][upright_parity] + step * here_lift
                put(3, lev, spot, here_up, change, mask)
                put(4, lev, spot, here_lift, -step * here_up, mask)
                if x > 0:
                    mass[1 - parity] = mass[1 - parity] - here_flow
                    flow[1 - parity] = flow[1 - parity] - here_mass
                if z > 0:
                    other = 1 - upright_parity
                    up_mass[x][other] = up_mass[x][other] - here_up
                    up_flow[x][other] = up_flow[x][other] - here_mass


def prepare(old_count, new_count, order, neighbour, face_code, own, near, far_left, far_right, shared, sems):
    tail = pl.multiple_of((old_count[0] - FAR) * ROWS, 8)
    copies = [
        pltpu.make_async_copy(own.at[: HELD * ROWS], near.at[: HELD * ROWS], sems.at[0]),
        pltpu.make_async_copy(own.at[pl.ds(tail, FAR * ROWS)], far_right.at[: FAR * ROWS], sems.at[1]),
        pltpu.make_async_copy(own.at[: FAR * ROWS], far_left.at[: FAR * ROWS], sems.at[2]),
    ]
    for copy in copies:
        copy.start()
    lane = lax.broadcasted_iota(jnp.int32, (1, LANES), 1)
    counts = jnp.where(lane == 0, old_count[0], jnp.where(lane == 1, new_count[0], 0))
    shared[...] = jnp.broadcast_to(counts[:, :2].reshape(1, 1, 2), shared.shape)
    wide = jnp.zeros((1, LANES - CAP), jnp.int32)
    orders = jnp.concatenate([order[...], wide], axis=1)
    wide = jnp.zeros((4, LANES - CAP), jnp.int32)
    rows = [
        jnp.concatenate([neighbour[...], wide], axis=1),
        jnp.concatenate([face_code[...], wide], axis=1),
        orders,
        counts,
        jnp.zeros((6, LANES), jnp.int32),
    ]
    near[HELD * ROWS :, :] = jnp.concatenate(rows, axis=0).astype(jnp.float32)
    orders = jnp.broadcast_to(orders, (8, LANES))
    far_left[FAR * ROWS :, :] = orders.astype(jnp.float32)
    last = pltpu.roll(orders, jnp.bitwise_and(16 - new_count[0], LANES - 1), 1)
    far_right[FAR * ROWS :, :] = last.astype(jnp.float32)
    for copy in copies:
        copy.wait()


def pack(old_count, new_count, order, neighbour, face_code, own, shards):
    smem = pl.BlockSpec(memory_space=pltpu.SMEM)
    vmem = pl.BlockSpec(memory_space=pltpu.VMEM)
    hbm = pl.BlockSpec(memory_space=pltpu.HBM)
    return pl.pallas_call(
        prepare,
        out_shape=(
            jax.ShapeDtypeStruct((HELD * ROWS + 16, LANES), jnp.float32),
            jax.ShapeDtypeStruct((FAR * ROWS + 8, LANES), jnp.float32),
            jax.ShapeDtypeStruct((FAR * ROWS + 8, LANES), jnp.float32),
            jax.ShapeDtypeStruct((shards, 1, 2), jnp.int32),
        ),
        in_specs=[smem, smem, vmem, vmem, vmem, hbm],
        out_specs=(vmem, vmem, vmem, vmem),
        scratch_shapes=[pltpu.SemaphoreType.DMA((3,))],
        name="pack",
    )(old_count, new_count, order, neighbour, face_code, own)


def body(
    place,
    old_count,
    new_count,
    table_left,
    table_right,
    shared,
    near,
    near_left,
    near_right,
    order_left,
    order_right,
    own,
    left,
    right,
    far_left,
    far_right,
    out,
    win,
    start,
    first,
    rise,
    fall,
    lift,
    side,
    sems,
):
    row = lax.broadcasted_iota(jnp.int32, shared.shape, 0)
    earlier = jnp.sum(jnp.where(row < place[0], shared[...], 0), axis=0)
    column = lax.broadcasted_iota(jnp.int32, (1, 2), 1)
    old_begin = jnp.sum(jnp.where(column == 0, earlier, 0))
    new_begin = jnp.sum(jnp.where(column == 1, earlier, 0))
    row_lane = lax.broadcasted_iota(jnp.int32, (1, LANES), 1)
    own_count, own_new = old_count[0], new_count[0]
    left_count, left_new = table_left[1, 0].astype(jnp.int32), table_left[1, 1].astype(jnp.int32)
    right_count, right_new = table_right[1, 0].astype(jnp.int32), table_right[1, 1].astype(jnp.int32)
    shift = REACH + old_begin - new_begin
    copies = fetch(
        win, sems, own, left, right, far_left, far_right, shift, own_count, left_count, right_count
    )
    for copy in copies:
        copy.start()
    lane = lax.broadcasted_iota(jnp.int32, (16, LANES), 1)
    after = REACH + own_new
    before = REACH - left_new

    def turn(values, amount):
        return pltpu.roll(values, jnp.bitwise_and(amount, LANES - 1), 1)

    window = jnp.where(
        lane < REACH,
        turn(near_left[...], before),
        jnp.where(lane < after, turn(near[...], REACH), turn(near_right[...], after)),
    )
    window = window.astype(jnp.int32)
    order = window[8:16, :][0:1, :]
    far_before = turn(order_left[...], before - 16)[0:1, :].astype(jnp.int32)
    far_after = turn(order_right[...], after + right_new)[0:1, :].astype(jnp.int32)
    order = jnp.where(row_lane < before, far_before, order)
    order = jnp.where(row_lane >= after + right_new, far_after, order)
    order = jnp.broadcast_to(order, (8, LANES))
    minor = lax.broadcasted_iota(jnp.int32, (8, LANES), 0)
    lane8 = lax.broadcasted_iota(jnp.int32, (8, LANES), 1)
    masks = [(jnp.maximum(minor, n) <= order).astype(jnp.float32) for n in range(8)]
    root = jnp.sqrt((2 * minor + 1).astype(jnp.float32))
    lanes, sources, signs = [], [], []
    for face in range(4):
        target = jnp.broadcast_to(window[face : face + 1, :], (8, LANES))
        code = jnp.broadcast_to(window[4 + face : 5 + face, :], (8, LANES))
        wall = target < 0
        lanes.append(jnp.bitwise_and(jnp.where(wall, lane8, target - new_begin + REACH), LANES - 1))
        sources.append(jnp.where(wall, face, code >> 1))
        odd = jnp.bitwise_and(code, 1) * jnp.bitwise_and(minor, 1)
        signs.append(jnp.where(wall, 1.0, 1.0 - 2.0 * odd.astype(jnp.float32)))
    for copy in copies:
        copy.wait()
    scaled = [masks[n] * root for n in range(8)]

    @pl.loop(0, 2)
    def _(lev):
        for field in range(5):
            for part in range(4):
                block = win[pl.ds(MARGIN * ROWS + field * 8 + part * 2 + lev, LANES, stride=ROWS), :].T
                for z in (2 * part, 2 * part + 1):
                    for x in range(8):
                        at = (z - 2 * part) * 64 + x * 8
                        value = block[at : at + 8, :] * scaled[max(z, x)] * (SCALE[z] * SCALE[x])
                        if field == 2:
                            start[field, lev, pl.ds(z * 64 + x, 8, stride=8), :] = value
                        else:
                            start[field, lev, pl.ds(z * 64 + x * 8, 8), :] = value

    section(start, None, first, rise, fall, lift, side, masks, lanes, sources, signs, False)
    section(first, start, start, rise, fall, lift, side, masks, lanes, sources, signs, True)
    valid = jnp.logical_and(lane8 >= REACH, lane8 < after)
    shrink = jnp.where(valid, 1.0 / root, 0.0)

    @pl.loop(0, 2)
    def _(lev):
        for field in range(5):
            for part in range(4):
                pieces = []
                for z in (2 * part, 2 * part + 1):
                    for x in range(8):
                        if field == 2:
                            value = start[field, lev, pl.ds(z * 64 + x, 8, stride=8), :]
                        else:
                            value = start[field, lev, pl.ds(z * 64 + x * 8, 8), :]
                        value = value * shrink * (1.0 / (SCALE[z] * SCALE[x]))
                        pieces.append(jnp.where(valid, value, 0.0))
                block = jnp.concatenate(pieces, axis=0).T
                out[pl.ds(field * 8 + part * 2 + lev, CAP, stride=ROWS), :] = block[REACH : REACH + CAP, :]


def advance(place, old_count, new_count, shared, near, near_left, near_right, own, far_left, far_right):
    smem = pl.BlockSpec(memory_space=pltpu.SMEM)
    vmem = pl.BlockSpec(memory_space=pltpu.VMEM)
    hbm = pl.BlockSpec(memory_space=pl.ANY)
    scalars = pl.BlockSpec((8, LANES), lambda i: (HELD * ROWS // 8 + 1, 0), memory_space=pltpu.SMEM)
    geometry = pl.BlockSpec((16, LANES), lambda i: (HELD * ROWS // 16, 0), memory_space=pltpu.VMEM)
    orders = pl.BlockSpec((8, LANES), lambda i: (FAR * ROWS // 8, 0), memory_space=pltpu.VMEM)
    return pl.pallas_call(
        body,
        grid=(1,),
        out_shape=jax.ShapeDtypeStruct((CAP * ROWS, LANES), jnp.float32),
        in_specs=[smem] * 3 + [scalars] * 2 + [vmem] + [geometry] * 3 + [orders] * 2 + [hbm] * 5,
        out_specs=vmem,
        scratch_shapes=[
            pltpu.VMEM(((MARGIN + LANES) * ROWS, LANES), jnp.float32),
            pltpu.VMEM((5, 2, 512, LANES), jnp.float32),
            pltpu.VMEM((5, 2, 512, LANES), jnp.float32),
            pltpu.VMEM((4, 2, 64, LANES), jnp.float32),
            pltpu.VMEM((4, 2, 64, LANES), jnp.float32),
            pltpu.VMEM((2, 2, 64, LANES), jnp.float32),
            pltpu.VMEM((512, LANES), jnp.float32),
            pltpu.SemaphoreType.DMA((5,)),
        ],
        compiler_params=pltpu.CompilerParams(vmem_limit_bytes=32 * 1024 * 1024),
        name="advance",
    )(
        place,
        old_count,
        new_count,
        near_left,
        near_right,
        shared,
        near,
        near_left,
        near_right,
        far_left,
        far_right,
        own,
        near_left,
        near_right,
        far_left,
        far_right,
    )


def local(old_state, old_count, new_count, column_order, neighbour, face_code):
    axes = ("grp", "dev")
    groups, members = lax.axis_size("grp"), lax.axis_size("dev")
    shards = groups * members
    here = lax.axis_index("grp") * members + lax.axis_index("dev")
    place = jnp.reshape(here, (1,)).astype(jnp.int32)

    def along(values, hop):
        return lax.ppermute(values, axes, [(i, (i + hop) % shards) for i in range(shards)])

    own = old_state.reshape(CAP, 5, 2, 4, LANES).transpose(0, 1, 3, 2, 4).reshape(CAP * ROWS, LANES)
    near, head, tail, shared = pack(
        old_count, new_count, column_order.reshape(1, CAP), neighbour, face_code, own, shards
    )
    near_left, near_right = along(near, 1), along(near, -1)
    far_left, far_right = along(tail, 2), along(head, -2)
    shared = lax.all_to_all(shared, axes, 0, 0, tiled=True)
    out = advance(
        place,
        old_count,
        new_count,
        shared,
        near,
        near_left,
        near_right,
        own,
        far_left,
        far_right,
    )
    out = out.reshape(CAP, 5, 4, 2, LANES).transpose(0, 1, 3, 2, 4)
    return out.reshape(CAP, 5, 2, 512)


def solution(mesh):
    in_specs = (
        P(("grp", "dev"), None, None, None),
        P(("grp", "dev")),
        P(("grp", "dev")),
        P(("grp", "dev")),
        P(None, ("grp", "dev")),
        P(None, ("grp", "dev")),
    )
    out_specs = P(("grp", "dev"), None, None, None)
    return jax.shard_map(local, mesh=mesh, in_specs=in_specs, out_specs=out_specs, check_vma=False)
```

```python
import jax
import jax.numpy as jnp
import numpy as np
from jax import lax
from jax.experimental import pallas as pl
from jax.experimental.pallas import tpu as pltpu
from jax.sharding import PartitionSpec as P

TIME_STEP = 0.005
CAP = 48
ROWS = 40
ORIGIN = 38
FAR = 10
HELD = 36
MARGIN = 8
KEPT = 64
LANES = 128
SCALE = [float(np.sqrt(2.0 * k + 1.0)) for k in range(8)]


def traces(state, lev, rise, fall):
    for z in range(8):
        along = [(0, 1), (2, 3)]
        for direction in range(2):
            sums = []
            for field in (0, 1 + direction):
                even = odd = None
                for k in range(8):
                    if direction == 0 or field == 2:
                        part = state[field, lev, pl.ds(z * 64 + k * 8, 8), :]
                    else:
                        part = state[field, lev, pl.ds(z * 64 + k, 8, stride=8), :]
                    if k == 0:
                        even = part
                    elif k == 1:
                        odd = part
                    elif k % 2 == 0:
                        even = even + part
                    else:
                        odd = odd + part
                sums.append((even - odd, even + odd))
            (mass_low, mass_high), (flow_low, flow_high) = sums
            low, high = along[direction]
            spot = pl.ds(z * 8, 8)
            rise[low, lev, spot, :] = mass_low - flow_low
            fall[low, lev, spot, :] = -flow_low - mass_low
            rise[high, lev, spot, :] = mass_high + flow_high
            fall[high, lev, spot, :] = flow_high - mass_high


def upright(state, lift):
    for x in range(8):
        ends = []
        for lev in range(2):
            sums = []
            for field in (0, 3):
                even = odd = None
                for z in range(8):
                    part = state[field, lev, pl.ds(z * 64 + x * 8, 8), :]
                    if z == 0:
                        even = part
                    elif z == 1:
                        odd = part
                    elif z % 2 == 0:
                        even = even + part
                    else:
                        odd = odd + part
                sums.append((even - odd, even + odd))
            ends.append(sums)
        ((mass_b0, mass_t0), (flow_b0, flow_t0)), ((mass_b1, mass_t1), (flow_b1, flow_t1)) = ends
        bottom0 = -2.0 * flow_b0
        top0 = (flow_t0 - mass_t0) + (mass_b1 - flow_b1)
        bottom1 = (mass_t0 + flow_t0) - (flow_b1 + mass_b1)
        top1 = 2.0 * flow_t1
        spot = pl.ds(x * 8, 8)
        lift[0, 0, spot, :] = 0.25 * (top0 + bottom0)
        lift[0, 1, spot, :] = 0.25 * (top0 - bottom0)
        lift[1, 0, spot, :] = 0.25 * (top1 + bottom1)
        lift[1, 1, spot, :] = 0.25 * (top1 - bottom1)


def jumps(lev, rise, fall, lanes, sources, signs, z):
    spot = pl.ds(z * 8, 8)
    parts = [rise[source, lev, spot, :] for source in range(4)]
    whole = []
    for face in range(4):
        picked = [
            jnp.take_along_axis(part, lanes[face], axis=1, mode="promise_in_bounds") for part in parts
        ]
        lower = jnp.where(sources[face] == 0, picked[0], picked[1])
        upper = jnp.where(sources[face] == 2, picked[2], picked[3])
        outer = jnp.where(sources[face] < 2, lower, upper)
        whole.append(fall[face, lev, spot, :] + signs[face] * outer)
    west, east, south, north = whole
    return (
        0.25 * (east + west),
        0.25 * (east - west),
        0.25 * (north + south),
        0.25 * (north - south),
    )


def section(state, base, result, rise, fall, lift, side, masks, lanes, sources, signs, last):
    step = TIME_STEP

    def put(field, lev, spot, old, change, mask):
        fresh = old + mask * change
        if last:
            fresh = 0.5 * base[field, lev, spot, :] + 0.5 * fresh
        result[field, lev, spot, :] = fresh

    upright(state, lift)

    @pl.loop(0, 2)
    def _(lev):
        traces(state, lev, rise, fall)
        tops = [[lift[lev, part, pl.ds(x * 8, 8), :] for x in range(8)] for part in range(2)]
        up_mass = [[tops[0][x], tops[1][x]] for x in range(8)]
        up_flow = [[-tops[1][x], -tops[0][x]] for x in range(8)]
        for z in reversed(range(8)):
            sum_x, diff_x, sum_y, diff_y = jumps(lev, rise, fall, lanes, sources, signs, z)
            mass = [sum_y, diff_y]
            flow = [-diff_y, -sum_y]
            for y in reversed(range(8)):
                spot = pl.ds(z * 64 + y * 8, 8)
                turned = pl.ds(z * 64 + y, 8, stride=8)
                parity = y % 2
                side[turned, :] = (step * 2.0 * (2 * y + 1)) * mass[parity]
                here_flow = state[2, lev, spot, :]
                put(2, lev, spot, here_flow, (step * 2.0 * (2 * y + 1)) * flow[parity], masks[max(z, y)])
                if y > 0:
                    mass[1 - parity] = mass[1 - parity] - here_flow
                    flow[1 - parity] = flow[1 - parity] - state[0, lev, turned, :]
            mass = [sum_x, diff_x]
            flow = [-diff_x, -sum_x]
            for x in reversed(range(8)):
                spot = pl.ds(z * 64 + x * 8, 8)
                parity, upright_parity = x % 2, z % 2
                mask = masks[max(z, x)]
                here_mass = state[0, lev, spot, :]
                here_flow = state[1, lev, spot, :]
                here_up = state[3, lev, spot, :]
                here_lift = state[4, lev, spot, :]
                change = (
                    (step * 2.0 * (2 * x + 1)) * mass[parity]
                    + (step * 4.0 * (2 * z + 1)) * up_mass[x][upright_parity]
                    + side[spot, :]
                )
                put(0, lev, spot, here_mass, change, mask)
                put(1, lev, spot, here_flow, (step * 2.0 * (2 * x + 1)) * flow[parity], mask)
                change = (step * 4.0 * (2 * z + 1)) * up_flow[x][upright_parity] + step * here_lift
                put(3, lev, spot, here_up, change, mask)
                put(4, lev, spot, here_lift, -step * here_up, mask)
                if x > 0:
                    mass[1 - parity] = mass[1 - parity] - here_flow
                    flow[1 - parity] = flow[1 - parity] - here_mass
                if z > 0:
                    other = 1 - upright_parity
                    up_mass[x][other] = up_mass[x][other] - here_up
                    up_flow[x][other] = up_flow[x][other] - here_mass


def prepare(old_count, new_count, geometry, own, near, far_left, far_right, shared):
    near[: HELD * ROWS, :] = own[: HELD * ROWS, :]
    far_left[: FAR * ROWS, :] = own[: FAR * ROWS, :]
    tail = pl.multiple_of((old_count[0] - FAR) * ROWS, 8)
    far_right[: FAR * ROWS, :] = own[pl.ds(tail, FAR * ROWS), :]
    lane = lax.broadcasted_iota(jnp.int32, (1, LANES), 1)
    counts = jnp.where(lane == 0, old_count[0], jnp.where(lane == 1, new_count[0], 0))
    shared[...] = jnp.broadcast_to(counts[:, :2].reshape(1, 1, 2), shared.shape)
    row = lax.broadcasted_iota(jnp.int32, (16, LANES), 0)
    near[META, :] = jnp.where(row == 9, counts, geometry[...]).astype(jnp.float32)
    orders = jnp.broadcast_to(geometry[8:9, :], (8, LANES))
    far_left[FAR * ROWS :, :] = orders.astype(jnp.float32)
    last = pltpu.roll(orders, jnp.bitwise_and(16 - new_count[0], LANES - 1), 1)
    far_right[FAR * ROWS :, :] = last.astype(jnp.float32)


def pack(old_count, new_count, geometry, own, shards):
    smem = pl.BlockSpec(memory_space=pltpu.SMEM)
    vmem = pl.BlockSpec(memory_space=pltpu.VMEM)
    return pl.pallas_call(
        prepare,
        out_shape=(
            jax.ShapeDtypeStruct((HELD * ROWS + 16, LANES), jnp.float32),
            jax.ShapeDtypeStruct((FAR * ROWS + 8, LANES), jnp.float32),
            jax.ShapeDtypeStruct((FAR * ROWS + 8, LANES), jnp.float32),
            jax.ShapeDtypeStruct((shards, 1, 2), jnp.int32),
        ),
        in_specs=[smem, smem, vmem, vmem],
        out_specs=(vmem, vmem, vmem, vmem),
        compiler_params=pltpu.CompilerParams(vmem_limit_bytes=8 * 1024 * 1024),
        name="pack",
    )(old_count, new_count, geometry, own)


META = pl.ds(HELD * ROWS, 16)


def entry(geometry, lane):
    row = geometry[9:10, :]
    at = lax.broadcasted_iota(jnp.int32, (1, LANES), 1) == lane
    return jnp.sum(jnp.where(at, row, 0.0)).astype(jnp.int32)


def assemble(old_count, own, left, right, far_left, far_right, turned, table, win):
    left_count, right_count = entry(left[META, :], 0), entry(right[META, :], 0)
    table[0:16, :] = own[META, :]
    table[16:32, :] = left[META, :]
    table[32:48, :] = right[META, :]
    table[48:56, :] = far_left[FAR * ROWS :, :]
    table[56:64, :] = far_right[FAR * ROWS :, :]

    def place(source, lane, count):
        spot = pl.ds(pl.multiple_of((lane + MARGIN) * ROWS, 8), count * ROWS)
        win[spot, :] = source[: count * ROWS, :]

    place(far_left, ORIGIN - left_count - FAR, FAR)
    place(left, ORIGIN - left_count, HELD)
    place(own, ORIGIN, HELD)
    place(right, ORIGIN + old_count[0], HELD)
    place(far_right, ORIGIN + old_count[0] + right_count, FAR)
    minor = lax.broadcasted_iota(jnp.int32, (8, LANES), 0)
    root = jnp.sqrt((2 * minor + 1).astype(jnp.float32))

    @pl.loop(0, 2)
    def _(lev):
        for field in range(5):
            for part in range(4):
                block = win[pl.ds(MARGIN * ROWS + field * 8 + part * 2 + lev, LANES, stride=ROWS), :].T
                for z in (2 * part, 2 * part + 1):
                    for x in range(8):
                        at = (z - 2 * part) * 64 + x * 8
                        value = block[at : at + 8, :] * root * (SCALE[z] * SCALE[x])
                        if field == 2:
                            turned[field, lev, pl.ds(z * 64 + x, 8, stride=8), :] = value
                        else:
                            turned[field, lev, pl.ds(z * 64 + x * 8, 8), :] = value


def gather(old_count, own, left, right, far_left, far_right):
    smem = pl.BlockSpec(memory_space=pltpu.SMEM)
    vmem = pl.BlockSpec(memory_space=pltpu.VMEM)
    return pl.pallas_call(
        assemble,
        grid=(1,),
        out_shape=(
            jax.ShapeDtypeStruct((5, 2, 512, LANES), jnp.float32),
            jax.ShapeDtypeStruct((64, LANES), jnp.float32),
        ),
        in_specs=[smem] + [vmem] * 5,
        out_specs=(vmem, vmem),
        scratch_shapes=[
            pltpu.VMEM(((MARGIN + LANES) * ROWS, LANES), jnp.float32),
        ],
        compiler_params=pltpu.CompilerParams(vmem_limit_bytes=14 * 1024 * 1024),
        cost_estimate=pl.CostEstimate(flops=1000000, bytes_accessed=6000000, transcendentals=0),
        name="gather",
    )(old_count, own, left, right, far_left, far_right)


def body(
    place,
    new_count,
    shared,
    table,
    state,
    out,
    start,
    first,
    rise,
    fall,
    lift,
    side,
    rows,
    sem,
):
    row = lax.broadcasted_iota(jnp.int32, shared.shape, 0)
    earlier = jnp.sum(jnp.where(row < place[0], shared[...], 0), axis=0)
    column = lax.broadcasted_iota(jnp.int32, (1, 2), 1)
    old_begin = jnp.sum(jnp.where(column == 0, earlier, 0))
    new_begin = jnp.sum(jnp.where(column == 1, earlier, 0))
    own_new = new_count[0]
    left_new, right_new = entry(table[16:32, :], 1), entry(table[32:48, :], 1)
    reach = new_begin - old_begin + ORIGIN
    after = reach + own_new
    before = reach - left_new
    lane = lax.broadcasted_iota(jnp.int32, (16, LANES), 1)
    row_lane = lax.broadcasted_iota(jnp.int32, (1, LANES), 1)

    def turn(values, amount):
        return pltpu.roll(values, jnp.bitwise_and(amount, LANES - 1), 1)

    window = jnp.where(
        lane < reach,
        turn(table[16:32, :], before),
        jnp.where(lane < after, turn(table[0:16, :], reach), turn(table[32:48, :], after)),
    )
    window = window.astype(jnp.int32)
    order = window[8:16, :][0:1, :]
    far_before = turn(table[48:56, :], before - 16)[0:1, :].astype(jnp.int32)
    far_after = turn(table[56:64, :], after + right_new)[0:1, :].astype(jnp.int32)
    order = jnp.where(row_lane < before, far_before, order)
    order = jnp.where(row_lane >= after + right_new, far_after, order)
    order = jnp.broadcast_to(order, (8, LANES))
    minor = lax.broadcasted_iota(jnp.int32, (8, LANES), 0)
    lane8 = lax.broadcasted_iota(jnp.int32, (8, LANES), 1)
    masks = [(jnp.maximum(minor, n) <= order).astype(jnp.float32) for n in range(8)]
    lanes, sources, signs = [], [], []
    for face in range(4):
        target = jnp.broadcast_to(window[face : face + 1, :], (8, LANES))
        code = jnp.broadcast_to(window[4 + face : 5 + face, :], (8, LANES))
        wall = target < 0
        lanes.append(jnp.bitwise_and(jnp.where(wall, lane8, target - old_begin + ORIGIN), LANES - 1))
        sources.append(jnp.where(wall, face, code >> 1))
        odd = jnp.bitwise_and(code, 1) * jnp.bitwise_and(minor, 1)
        signs.append(jnp.where(wall, 1.0, 1.0 - 2.0 * odd.astype(jnp.float32)))

    @pl.loop(0, 2)
    def _(lev):
        for field in range(5):
            for z in range(8):
                for x in range(8):
                    spot = pl.ds(z * 64 + x * 8, 8)
                    start[field, lev, spot, :] = state[field, lev, spot, :] * masks[max(z, x)]

    section(start, None, first, rise, fall, lift, side, masks, lanes, sources, signs, False)
    section(first, start, start, rise, fall, lift, side, masks, lanes, sources, signs, True)
    valid = jnp.logical_and(lane8 >= reach, lane8 < after)
    root = jnp.sqrt((2 * minor + 1).astype(jnp.float32))
    shrink = jnp.where(valid, 1.0 / root, 0.0)

    @pl.loop(0, 2)
    def _(lev):
        for field in range(5):
            for part in range(4):
                pieces = []
                for z in (2 * part, 2 * part + 1):
                    for x in range(8):
                        if field == 2:
                            value = start[field, lev, pl.ds(z * 64 + x, 8, stride=8), :]
                        else:
                            value = start[field, lev, pl.ds(z * 64 + x * 8, 8), :]
                        value = value * shrink * (1.0 / (SCALE[z] * SCALE[x]))
                        pieces.append(jnp.where(valid, value, 0.0))
                block = jnp.concatenate(pieces, axis=0).T
                kept = pl.ds(field * 8 + part * 2 + lev, KEPT, stride=ROWS)
                rows[kept, :] = block[32 : 32 + KEPT, :]

    first_row = pl.multiple_of((reach - 32) * ROWS, 8)
    copy = pltpu.make_async_copy(rows.at[pl.ds(first_row, CAP * ROWS)], out, sem)
    copy.start()
    copy.wait()


def advance(place, new_count, shared, table, state):
    smem = pl.BlockSpec(memory_space=pltpu.SMEM)
    vmem = pl.BlockSpec(memory_space=pltpu.VMEM)
    hbm = pl.BlockSpec(memory_space=pl.ANY)
    return pl.pallas_call(
        body,
        out_shape=jax.ShapeDtypeStruct((CAP * ROWS, LANES), jnp.float32),
        in_specs=[smem] * 2 + [vmem] * 3,
        out_specs=hbm,
        scratch_shapes=[
            pltpu.VMEM((5, 2, 512, LANES), jnp.float32),
            pltpu.VMEM((5, 2, 512, LANES), jnp.float32),
            pltpu.VMEM((4, 2, 64, LANES), jnp.float32),
            pltpu.VMEM((4, 2, 64, LANES), jnp.float32),
            pltpu.VMEM((2, 2, 64, LANES), jnp.float32),
            pltpu.VMEM((512, LANES), jnp.float32),
            pltpu.VMEM((KEPT * ROWS, LANES), jnp.float32),
            pltpu.SemaphoreType.DMA,
        ],
        compiler_params=pltpu.CompilerParams(vmem_limit_bytes=16 * 1024 * 1024),
        name="advance",
    )(
        place,
        new_count,
        shared,
        table,
        state,
    )


def local(old_state, old_count, new_count, column_order, neighbour, face_code):
    axes = ("grp", "dev")
    groups, members = lax.axis_size("grp"), lax.axis_size("dev")
    shards = groups * members
    here = lax.axis_index("grp") * members + lax.axis_index("dev")
    place = jnp.reshape(here, (1,)).astype(jnp.int32)

    def along(values, hop):
        return lax.ppermute(values, axes, [(i, (i + hop) % shards) for i in range(shards)])

    own = old_state.reshape(CAP, 5, 2, 4, LANES).transpose(0, 1, 3, 2, 4).reshape(CAP * ROWS, LANES)
    geometry = jnp.concatenate([neighbour, face_code, column_order[None, :]], axis=0)
    geometry = jnp.pad(geometry, ((0, 7), (0, LANES - CAP)))
    near, head, tail, shared = pack(old_count, new_count, geometry, own, shards)
    near_left, near_right = along(near, 1), along(near, -1)
    far_left, far_right = along(tail, 2), along(head, -2)
    shared = lax.all_to_all(shared, axes, 0, 0, tiled=True)
    state, table = gather(old_count, near, near_left, near_right, far_left, far_right)
    out = advance(place, new_count, shared, table, state)
    out = out.reshape(CAP, 5, 4, 2, LANES).transpose(0, 1, 3, 2, 4)
    return out.reshape(CAP, 5, 2, 512)


def solution(mesh):
    in_specs = (
        P(("grp", "dev"), None, None, None),
        P(("grp", "dev")),
        P(("grp", "dev")),
        P(("grp", "dev")),
        P(None, ("grp", "dev")),
        P(None, ("grp", "dev")),
    )
    out_specs = P(("grp", "dev"), None, None, None)
    return jax.shard_map(local, mesh=mesh, in_specs=in_specs, out_specs=out_specs, check_vma=False)
```

```python
import jax
import jax.numpy as jnp
import numpy as np
from jax import lax
from jax.experimental import pallas as pl
from jax.experimental.pallas import tpu as pltpu
from jax.sharding import PartitionSpec as P

TIME_STEP = 0.005
CAP = 48
ROWS = 40
ORIGIN = 38
FAR = 10
HELD = 36
MARGIN = 8
KEPT = 64
LANES = 128
SCALE = [float(np.sqrt(2.0 * k + 1.0)) for k in range(8)]


def traces(state, lev, rise, fall):
    for z in range(8):
        along = [(0, 1), (2, 3)]
        for direction in range(2):
            sums = []
            for field in (0, 1 + direction):
                even = odd = None
                for k in range(8):
                    if direction == 0 or field == 2:
                        part = state[field, lev, pl.ds(z * 64 + k * 8, 8), :]
                    else:
                        part = state[field, lev, pl.ds(z * 64 + k, 8, stride=8), :]
                    if k == 0:
                        even = part
                    elif k == 1:
                        odd = part
                    elif k % 2 == 0:
                        even = even + part
                    else:
                        odd = odd + part
                sums.append((even - odd, even + odd))
            (mass_low, mass_high), (flow_low, flow_high) = sums
            low, high = along[direction]
            spot = pl.ds(z * 8, 8)
            rise[low, lev, spot, :] = mass_low - flow_low
            fall[low, lev, spot, :] = -flow_low - mass_low
            rise[high, lev, spot, :] = mass_high + flow_high
            fall[high, lev, spot, :] = flow_high - mass_high


def upright(state, lift):
    for x in range(8):
        ends = []
        for lev in range(2):
            sums = []
            for field in (0, 3):
                even = odd = None
                for z in range(8):
                    part = state[field, lev, pl.ds(z * 64 + x * 8, 8), :]
                    if z == 0:
                        even = part
                    elif z == 1:
                        odd = part
                    elif z % 2 == 0:
                        even = even + part
                    else:
                        odd = odd + part
                sums.append((even - odd, even + odd))
            ends.append(sums)
        ((mass_b0, mass_t0), (flow_b0, flow_t0)), ((mass_b1, mass_t1), (flow_b1, flow_t1)) = ends
        bottom0 = -2.0 * flow_b0
        top0 = (flow_t0 - mass_t0) + (mass_b1 - flow_b1)
        bottom1 = (mass_t0 + flow_t0) - (flow_b1 + mass_b1)
        top1 = 2.0 * flow_t1
        spot = pl.ds(x * 8, 8)
        lift[0, 0, spot, :] = 0.25 * (top0 + bottom0)
        lift[0, 1, spot, :] = 0.25 * (top0 - bottom0)
        lift[1, 0, spot, :] = 0.25 * (top1 + bottom1)
        lift[1, 1, spot, :] = 0.25 * (top1 - bottom1)


def jumps(lev, rise, fall, lanes, sources, signs, z):
    spot = pl.ds(z * 8, 8)
    parts = [rise[source, lev, spot, :] for source in range(4)]
    whole = []
    for face in range(4):
        picked = [
            jnp.take_along_axis(part, lanes[face], axis=1, mode="promise_in_bounds") for part in parts
        ]
        lower = jnp.where(sources[face] == 0, picked[0], picked[1])
        upper = jnp.where(sources[face] == 2, picked[2], picked[3])
        outer = jnp.where(sources[face] < 2, lower, upper)
        whole.append(fall[face, lev, spot, :] + signs[face] * outer)
    west, east, south, north = whole
    return (
        0.25 * (east + west),
        0.25 * (east - west),
        0.25 * (north + south),
        0.25 * (north - south),
    )


def section(state, base, result, rise, fall, lift, side, masks, lanes, sources, signs, last):
    step = TIME_STEP

    def put(field, lev, spot, old, change, mask):
        fresh = old + mask * change
        if last:
            fresh = 0.5 * base[field, lev, spot, :] + 0.5 * fresh
        result[field, lev, spot, :] = fresh

    upright(state, lift)

    @pl.loop(0, 2)
    def _(lev):
        traces(state, lev, rise, fall)
        tops = [[lift[lev, part, pl.ds(x * 8, 8), :] for x in range(8)] for part in range(2)]
        up_mass = [[tops[0][x], tops[1][x]] for x in range(8)]
        up_flow = [[-tops[1][x], -tops[0][x]] for x in range(8)]
        for z in reversed(range(8)):
            sum_x, diff_x, sum_y, diff_y = jumps(lev, rise, fall, lanes, sources, signs, z)
            mass = [sum_y, diff_y]
            flow = [-diff_y, -sum_y]
            for y in reversed(range(8)):
                spot = pl.ds(z * 64 + y * 8, 8)
                turned = pl.ds(z * 64 + y, 8, stride=8)
                parity = y % 2
                side[turned, :] = (step * 2.0 * (2 * y + 1)) * mass[parity]
                here_flow = state[2, lev, spot, :]
                put(2, lev, spot, here_flow, (step * 2.0 * (2 * y + 1)) * flow[parity], masks[max(z, y)])
                if y > 0:
                    mass[1 - parity] = mass[1 - parity] - here_flow
                    flow[1 - parity] = flow[1 - parity] - state[0, lev, turned, :]
            mass = [sum_x, diff_x]
            flow = [-diff_x, -sum_x]
            for x in reversed(range(8)):
                spot = pl.ds(z * 64 + x * 8, 8)
                parity, upright_parity = x % 2, z % 2
                mask = masks[max(z, x)]
                here_mass = state[0, lev, spot, :]
                here_flow = state[1, lev, spot, :]
                here_up = state[3, lev, spot, :]
                here_lift = state[4, lev, spot, :]
                change = (
                    (step * 2.0 * (2 * x + 1)) * mass[parity]
                    + (step * 4.0 * (2 * z + 1)) * up_mass[x][upright_parity]
                    + side[spot, :]
                )
                put(0, lev, spot, here_mass, change, mask)
                put(1, lev, spot, here_flow, (step * 2.0 * (2 * x + 1)) * flow[parity], mask)
                change = (step * 4.0 * (2 * z + 1)) * up_flow[x][upright_parity] + step * here_lift
                put(3, lev, spot, here_up, change, mask)
                put(4, lev, spot, here_lift, -step * here_up, mask)
                if x > 0:
                    mass[1 - parity] = mass[1 - parity] - here_flow
                    flow[1 - parity] = flow[1 - parity] - here_mass
                if z > 0:
                    other = 1 - upright_parity
                    up_mass[x][other] = up_mass[x][other] - here_up
                    up_flow[x][other] = up_flow[x][other] - here_mass


def prepare(old_count, new_count, sibling, geometry, own, near, far_left, far_right, shared):
    near[: HELD * ROWS, :] = own[: HELD * ROWS, :]
    far_left[: FAR * ROWS, :] = own[: FAR * ROWS, :]
    tail = pl.multiple_of((old_count[0] - FAR) * ROWS, 8)
    far_right[: FAR * ROWS, :] = own[pl.ds(tail, FAR * ROWS), :]
    lane = lax.broadcasted_iota(jnp.int32, (1, LANES), 1)
    counts = jnp.where(lane == 0, old_count[0], jnp.where(lane == 1, new_count[0], 0))
    both = counts + jnp.where(lane == 0, sibling[0], jnp.where(lane == 1, sibling[1], 0))
    shared[...] = jnp.broadcast_to(both[:, :2].reshape(1, 1, 2), shared.shape)
    row = lax.broadcasted_iota(jnp.int32, (16, LANES), 0)
    near[META, :] = jnp.where(row == 9, counts, geometry[...]).astype(jnp.float32)
    orders = jnp.broadcast_to(geometry[8:9, :], (8, LANES))
    far_left[FAR * ROWS :, :] = orders.astype(jnp.float32)
    last = pltpu.roll(orders, jnp.bitwise_and(16 - new_count[0], LANES - 1), 1)
    far_right[FAR * ROWS :, :] = last.astype(jnp.float32)


def pack(old_count, new_count, sibling, geometry, own, shards):
    smem = pl.BlockSpec(memory_space=pltpu.SMEM)
    vmem = pl.BlockSpec(memory_space=pltpu.VMEM)
    return pl.pallas_call(
        prepare,
        out_shape=(
            jax.ShapeDtypeStruct((HELD * ROWS + 16, LANES), jnp.float32),
            jax.ShapeDtypeStruct((FAR * ROWS + 8, LANES), jnp.float32),
            jax.ShapeDtypeStruct((FAR * ROWS + 8, LANES), jnp.float32),
            jax.ShapeDtypeStruct((shards // 2, 1, 2), jnp.int32),
        ),
        in_specs=[smem, smem, smem, vmem, vmem],
        out_specs=(vmem, vmem, vmem, vmem),
        compiler_params=pltpu.CompilerParams(vmem_limit_bytes=8 * 1024 * 1024),
        name="pack",
    )(old_count, new_count, sibling, geometry, own)


META = pl.ds(HELD * ROWS, 16)


def entry(geometry, lane):
    row = geometry[9:10, :]
    at = lax.broadcasted_iota(jnp.int32, (1, LANES), 1) == lane
    return jnp.sum(jnp.where(at, row, 0.0)).astype(jnp.int32)


def assemble(old_count, own, left, right, far_left, far_right, turned, table, win):
    left_count, right_count = entry(left[META, :], 0), entry(right[META, :], 0)
    table[0:16, :] = own[META, :]
    table[16:32, :] = left[META, :]
    table[32:48, :] = right[META, :]
    table[48:56, :] = far_left[FAR * ROWS :, :]
    table[56:64, :] = far_right[FAR * ROWS :, :]

    def place(source, lane, count):
        spot = pl.ds(pl.multiple_of((lane + MARGIN) * ROWS, 8), count * ROWS)
        win[spot, :] = source[: count * ROWS, :]

    place(far_left, ORIGIN - left_count - FAR, FAR)
    place(left, ORIGIN - left_count, HELD)
    place(own, ORIGIN, HELD)
    place(right, ORIGIN + old_count[0], HELD)
    place(far_right, ORIGIN + old_count[0] + right_count, FAR)
    minor = lax.broadcasted_iota(jnp.int32, (8, LANES), 0)
    root = jnp.sqrt((2 * minor + 1).astype(jnp.float32))

    @pl.loop(0, 2)
    def _(lev):
        for field in range(5):
            for part in range(4):
                block = win[pl.ds(MARGIN * ROWS + field * 8 + part * 2 + lev, LANES, stride=ROWS), :].T
                for z in (2 * part, 2 * part + 1):
                    for x in range(8):
                        at = (z - 2 * part) * 64 + x * 8
                        value = block[at : at + 8, :] * root * (SCALE[z] * SCALE[x])
                        if field == 2:
                            turned[field, lev, pl.ds(z * 64 + x, 8, stride=8), :] = value
                        else:
                            turned[field, lev, pl.ds(z * 64 + x * 8, 8), :] = value


def gather(old_count, own, left, right, far_left, far_right):
    smem = pl.BlockSpec(memory_space=pltpu.SMEM)
    vmem = pl.BlockSpec(memory_space=pltpu.VMEM)
    return pl.pallas_call(
        assemble,
        grid=(1,),
        out_shape=(
            jax.ShapeDtypeStruct((5, 2, 512, LANES), jnp.float32),
            jax.ShapeDtypeStruct((64, LANES), jnp.float32),
        ),
        in_specs=[smem] + [vmem] * 5,
        out_specs=(vmem, vmem),
        scratch_shapes=[
            pltpu.VMEM(((MARGIN + LANES) * ROWS, LANES), jnp.float32),
        ],
        compiler_params=pltpu.CompilerParams(vmem_limit_bytes=14 * 1024 * 1024),
        cost_estimate=pl.CostEstimate(flops=1000000, bytes_accessed=6000000, transcendentals=0),
        name="gather",
    )(old_count, own, left, right, far_left, far_right)


def body(
    place,
    new_count,
    shared,
    table,
    state,
    out,
    start,
    first,
    rise,
    fall,
    lift,
    side,
    rows,
    sem,
):
    row = lax.broadcasted_iota(jnp.int32, shared.shape, 0)
    earlier = jnp.sum(jnp.where(row < place[0] >> 1, shared[...], 0), axis=0)
    column = lax.broadcasted_iota(jnp.int32, (1, 2), 1)
    second = jnp.bitwise_and(place[0], 1)
    left_old = entry(table[16:32, :], 0)
    left_new, right_new = entry(table[16:32, :], 1), entry(table[32:48, :], 1)
    old_begin = jnp.sum(jnp.where(column == 0, earlier, 0)) + second * left_old
    new_begin = jnp.sum(jnp.where(column == 1, earlier, 0)) + second * left_new
    own_new = new_count[0]
    reach = new_begin - old_begin + ORIGIN
    after = reach + own_new
    before = reach - left_new
    lane = lax.broadcasted_iota(jnp.int32, (16, LANES), 1)
    row_lane = lax.broadcasted_iota(jnp.int32, (1, LANES), 1)

    def turn(values, amount):
        return pltpu.roll(values, jnp.bitwise_and(amount, LANES - 1), 1)

    window = jnp.where(
        lane < reach,
        turn(table[16:32, :], before),
        jnp.where(lane < after, turn(table[0:16, :], reach), turn(table[32:48, :], after)),
    )
    window = window.astype(jnp.int32)
    order = window[8:16, :][0:1, :]
    far_before = turn(table[48:56, :], before - 16)[0:1, :].astype(jnp.int32)
    far_after = turn(table[56:64, :], after + right_new)[0:1, :].astype(jnp.int32)
    order = jnp.where(row_lane < before, far_before, order)
    order = jnp.where(row_lane >= after + right_new, far_after, order)
    order = jnp.broadcast_to(order, (8, LANES))
    minor = lax.broadcasted_iota(jnp.int32, (8, LANES), 0)
    lane8 = lax.broadcasted_iota(jnp.int32, (8, LANES), 1)
    masks = [(jnp.maximum(minor, n) <= order).astype(jnp.float32) for n in range(8)]
    lanes, sources, signs = [], [], []
    for face in range(4):
        target = jnp.broadcast_to(window[face : face + 1, :], (8, LANES))
        code = jnp.broadcast_to(window[4 + face : 5 + face, :], (8, LANES))
        wall = target < 0
        lanes.append(jnp.bitwise_and(jnp.where(wall, lane8, target - old_begin + ORIGIN), LANES - 1))
        sources.append(jnp.where(wall, face, code >> 1))
        odd = jnp.bitwise_and(code, 1) * jnp.bitwise_and(minor, 1)
        signs.append(jnp.where(wall, 1.0, 1.0 - 2.0 * odd.astype(jnp.float32)))

    @pl.loop(0, 2)
    def _(lev):
        for field in range(5):
            for z in range(8):
                for x in range(8):
                    spot = pl.ds(z * 64 + x * 8, 8)
                    start[field, lev, spot, :] = state[field, lev, spot, :] * masks[max(z, x)]

    section(start, None, first, rise, fall, lift, side, masks, lanes, sources, signs, False)
    section(first, start, start, rise, fall, lift, side, masks, lanes, sources, signs, True)
    valid = jnp.logical_and(lane8 >= reach, lane8 < after)
    root = jnp.sqrt((2 * minor + 1).astype(jnp.float32))
    shrink = jnp.where(valid, 1.0 / root, 0.0)

    @pl.loop(0, 2)
    def _(lev):
        for field in range(5):
            for part in range(4):
                pieces = []
                for z in (2 * part, 2 * part + 1):
                    for x in range(8):
                        if field == 2:
                            value = start[field, lev, pl.ds(z * 64 + x, 8, stride=8), :]
                        else:
                            value = start[field, lev, pl.ds(z * 64 + x * 8, 8), :]
                        value = value * shrink * (1.0 / (SCALE[z] * SCALE[x]))
                        pieces.append(jnp.where(valid, value, 0.0))
                block = jnp.concatenate(pieces, axis=0).T
                kept = pl.ds(field * 8 + part * 2 + lev, KEPT, stride=ROWS)
                rows[kept, :] = block[32 : 32 + KEPT, :]

    first_row = pl.multiple_of((reach - 32) * ROWS, 8)
    copy = pltpu.make_async_copy(rows.at[pl.ds(first_row, CAP * ROWS)], out, sem)
    copy.start()
    copy.wait()


def advance(place, new_count, shared, table, state):
    smem = pl.BlockSpec(memory_space=pltpu.SMEM)
    vmem = pl.BlockSpec(memory_space=pltpu.VMEM)
    hbm = pl.BlockSpec(memory_space=pl.ANY)
    return pl.pallas_call(
        body,
        out_shape=jax.ShapeDtypeStruct((CAP * ROWS, LANES), jnp.float32),
        in_specs=[smem] * 2 + [vmem] * 3,
        out_specs=hbm,
        scratch_shapes=[
            pltpu.VMEM((5, 2, 512, LANES), jnp.float32),
            pltpu.VMEM((5, 2, 512, LANES), jnp.float32),
            pltpu.VMEM((4, 2, 64, LANES), jnp.float32),
            pltpu.VMEM((4, 2, 64, LANES), jnp.float32),
            pltpu.VMEM((2, 2, 64, LANES), jnp.float32),
            pltpu.VMEM((512, LANES), jnp.float32),
            pltpu.VMEM((KEPT * ROWS, LANES), jnp.float32),
            pltpu.SemaphoreType.DMA,
        ],
        compiler_params=pltpu.CompilerParams(vmem_limit_bytes=16 * 1024 * 1024),
        name="advance",
    )(
        place,
        new_count,
        shared,
        table,
        state,
    )


def local(old_state, old_count, new_count, column_order, neighbour, face_code):
    axes = ("grp", "dev")
    groups, members = lax.axis_size("grp"), lax.axis_size("dev")
    shards = groups * members
    here = lax.axis_index("grp") * members + lax.axis_index("dev")
    place = jnp.reshape(here, (1,)).astype(jnp.int32)

    def along(values, hop):
        return lax.ppermute(values, axes, [(i, (i + hop) % shards) for i in range(shards)])

    own = old_state.reshape(CAP, 5, 2, 4, LANES).transpose(0, 1, 3, 2, 4).reshape(CAP * ROWS, LANES)
    counts = jnp.concatenate([old_count, new_count])
    sibling = lax.ppermute(counts, axes, [(i, i ^ 1) for i in range(shards)])
    geometry = jnp.concatenate([neighbour, face_code, column_order[None, :]], axis=0)
    geometry = jnp.pad(geometry, ((0, 7), (0, LANES - CAP)))
    near, head, tail, shared = pack(old_count, new_count, sibling, geometry, own, shards)
    near_left, near_right = along(near, 1), along(near, -1)
    far_left, far_right = along(tail, 2), along(head, -2)
    cores = [[2 * pair + core for pair in range(shards // 2)] for core in range(2)]
    shared = lax.all_to_all(shared, axes, 0, 0, axis_index_groups=cores, tiled=True)
    state, table = gather(old_count, near, near_left, near_right, far_left, far_right)
    out = advance(place, new_count, shared, table, state)
    out = out.reshape(CAP, 5, 4, 2, LANES).transpose(0, 1, 3, 2, 4)
    return out.reshape(CAP, 5, 2, 512)


def solution(mesh):
    in_specs = (
        P(("grp", "dev"), None, None, None),
        P(("grp", "dev")),
        P(("grp", "dev")),
        P(("grp", "dev")),
        P(None, ("grp", "dev")),
        P(None, ("grp", "dev")),
    )
    out_specs = P(("grp", "dev"), None, None, None)
    return jax.shard_map(local, mesh=mesh, in_specs=in_specs, out_specs=out_specs, check_vma=False)
```

```python
import jax
import jax.numpy as jnp
import numpy as np
from jax import lax
from jax.experimental import pallas as pl
from jax.experimental.pallas import tpu as pltpu
from jax.sharding import PartitionSpec as P

TIME_STEP = 0.005
CAP = 48
ROWS = 40
ORIGIN = 38
FAR = 10
HELD = 36
MARGIN = 8
KEPT = 64
LANES = 128
SCALE = [float(np.sqrt(2.0 * k + 1.0)) for k in range(8)]


def traces(state, lev, rise, fall):
    for z in range(8):
        along = [(0, 1), (2, 3)]
        for direction in range(2):
            sums = []
            for field in (0, 1 + direction):
                even = odd = None
                for k in range(8):
                    if direction == 0 or field == 2:
                        part = state[field, lev, pl.ds(z * 64 + k * 8, 8), :]
                    else:
                        part = state[field, lev, pl.ds(z * 64 + k, 8, stride=8), :]
                    if k == 0:
                        even = part
                    elif k == 1:
                        odd = part
                    elif k % 2 == 0:
                        even = even + part
                    else:
                        odd = odd + part
                sums.append((even - odd, even + odd))
            (mass_low, mass_high), (flow_low, flow_high) = sums
            low, high = along[direction]
            spot = pl.ds(z * 8, 8)
            rise[low, lev, spot, :] = mass_low - flow_low
            fall[low, lev, spot, :] = -flow_low - mass_low
            rise[high, lev, spot, :] = mass_high + flow_high
            fall[high, lev, spot, :] = flow_high - mass_high


def upright(state, lift):
    for x in range(8):
        ends = []
        for lev in range(2):
            sums = []
            for field in (0, 3):
                even = odd = None
                for z in range(8):
                    part = state[field, lev, pl.ds(z * 64 + x * 8, 8), :]
                    if z == 0:
                        even = part
                    elif z == 1:
                        odd = part
                    elif z % 2 == 0:
                        even = even + part
                    else:
                        odd = odd + part
                sums.append((even - odd, even + odd))
            ends.append(sums)
        ((mass_b0, mass_t0), (flow_b0, flow_t0)), ((mass_b1, mass_t1), (flow_b1, flow_t1)) = ends
        bottom0 = -2.0 * flow_b0
        top0 = (flow_t0 - mass_t0) + (mass_b1 - flow_b1)
        bottom1 = (mass_t0 + flow_t0) - (flow_b1 + mass_b1)
        top1 = 2.0 * flow_t1
        spot = pl.ds(x * 8, 8)
        lift[0, 0, spot, :] = 0.25 * (top0 + bottom0)
        lift[0, 1, spot, :] = 0.25 * (top0 - bottom0)
        lift[1, 0, spot, :] = 0.25 * (top1 + bottom1)
        lift[1, 1, spot, :] = 0.25 * (top1 - bottom1)


def jumps(lev, rise, fall, lanes, sources, signs, z):
    spot = pl.ds(z * 8, 8)
    parts = [rise[source, lev, spot, :] for source in range(4)]
    whole = []
    for face in range(4):
        picked = [
            jnp.take_along_axis(part, lanes[face], axis=1, mode="promise_in_bounds") for part in parts
        ]
        lower = jnp.where(sources[face] == 0, picked[0], picked[1])
        upper = jnp.where(sources[face] == 2, picked[2], picked[3])
        outer = jnp.where(sources[face] < 2, lower, upper)
        whole.append(fall[face, lev, spot, :] + signs[face] * outer)
    west, east, south, north = whole
    return (
        0.25 * (east + west),
        0.25 * (east - west),
        0.25 * (north + south),
        0.25 * (north - south),
    )


def section(state, base, result, rise, fall, lift, side, masks, lanes, sources, signs, last):
    step = TIME_STEP

    def put(field, lev, spot, old, change, mask):
        fresh = old + mask * change
        if last:
            fresh = 0.5 * base[field, lev, spot, :] + 0.5 * fresh
        result[field, lev, spot, :] = fresh

    upright(state, lift)

    @pl.loop(0, 2)
    def _(lev):
        traces(state, lev, rise, fall)
        tops = [[lift[lev, part, pl.ds(x * 8, 8), :] for x in range(8)] for part in range(2)]
        up_mass = [[tops[0][x], tops[1][x]] for x in range(8)]
        up_flow = [[-tops[1][x], -tops[0][x]] for x in range(8)]
        for z in reversed(range(8)):
            sum_x, diff_x, sum_y, diff_y = jumps(lev, rise, fall, lanes, sources, signs, z)
            mass = [sum_y, diff_y]
            flow = [-diff_y, -sum_y]
            for y in reversed(range(8)):
                spot = pl.ds(z * 64 + y * 8, 8)
                turned = pl.ds(z * 64 + y, 8, stride=8)
                parity = y % 2
                side[turned, :] = (step * 2.0 * (2 * y + 1)) * mass[parity]
                here_flow = state[2, lev, spot, :]
                put(2, lev, spot, here_flow, (step * 2.0 * (2 * y + 1)) * flow[parity], masks[max(z, y)])
                if y > 0:
                    mass[1 - parity] = mass[1 - parity] - here_flow
                    flow[1 - parity] = flow[1 - parity] - state[0, lev, turned, :]
            mass = [sum_x, diff_x]
            flow = [-diff_x, -sum_x]
            for x in reversed(range(8)):
                spot = pl.ds(z * 64 + x * 8, 8)
                parity, upright_parity = x % 2, z % 2
                mask = masks[max(z, x)]
                here_mass = state[0, lev, spot, :]
                here_flow = state[1, lev, spot, :]
                here_up = state[3, lev, spot, :]
                here_lift = state[4, lev, spot, :]
                change = (
                    (step * 2.0 * (2 * x + 1)) * mass[parity]
                    + (step * 4.0 * (2 * z + 1)) * up_mass[x][upright_parity]
                    + side[spot, :]
                )
                put(0, lev, spot, here_mass, change, mask)
                put(1, lev, spot, here_flow, (step * 2.0 * (2 * x + 1)) * flow[parity], mask)
                change = (step * 4.0 * (2 * z + 1)) * up_flow[x][upright_parity] + step * here_lift
                put(3, lev, spot, here_up, change, mask)
                put(4, lev, spot, here_lift, -step * here_up, mask)
                if x > 0:
                    mass[1 - parity] = mass[1 - parity] - here_flow
                    flow[1 - parity] = flow[1 - parity] - here_mass
                if z > 0:
                    other = 1 - upright_parity
                    up_mass[x][other] = up_mass[x][other] - here_up
                    up_flow[x][other] = up_flow[x][other] - here_mass


def prepare(old_count, new_count, sibling, geometry, own, near, far_left, far_right):
    near[: HELD * ROWS, :] = own[: HELD * ROWS, :]
    far_left[: FAR * ROWS, :] = own[: FAR * ROWS, :]
    tail = pl.multiple_of((old_count[0] - FAR) * ROWS, 8)
    far_right[: FAR * ROWS, :] = own[pl.ds(tail, FAR * ROWS), :]
    lane = lax.broadcasted_iota(jnp.int32, (1, LANES), 1)
    counts = jnp.where(lane == 0, old_count[0], jnp.where(lane == 1, new_count[0], 0))
    row = lax.broadcasted_iota(jnp.int32, (16, LANES), 0)
    near[META, :] = jnp.where(row == 9, counts, geometry[...]).astype(jnp.float32)
    orders = jnp.broadcast_to(geometry[8:9, :], (8, LANES))
    far_left[FAR * ROWS :, :] = orders.astype(jnp.float32)
    last = pltpu.roll(orders, jnp.bitwise_and(16 - new_count[0], LANES - 1), 1)
    far_right[FAR * ROWS :, :] = last.astype(jnp.float32)


def pack(old_count, new_count, sibling, geometry, own):
    smem = pl.BlockSpec(memory_space=pltpu.SMEM)
    vmem = pl.BlockSpec(memory_space=pltpu.VMEM)
    return pl.pallas_call(
        prepare,
        out_shape=(
            jax.ShapeDtypeStruct((HELD * ROWS + 16, LANES), jnp.float32),
            jax.ShapeDtypeStruct((FAR * ROWS + 8, LANES), jnp.float32),
            jax.ShapeDtypeStruct((FAR * ROWS + 8, LANES), jnp.float32),
        ),
        in_specs=[smem, smem, pl.BlockSpec(memory_space=pl.ANY), vmem, vmem],
        out_specs=(vmem, vmem, vmem),
        compiler_params=pltpu.CompilerParams(vmem_limit_bytes=8 * 1024 * 1024),
        name="pack",
    )(old_count, new_count, sibling, geometry, own)


META = pl.ds(HELD * ROWS, 16)


def entry(geometry, lane):
    row = geometry[9:10, :]
    at = lax.broadcasted_iota(jnp.int32, (1, LANES), 1) == lane
    return jnp.sum(jnp.where(at, row, 0.0)).astype(jnp.int32)


def assemble(old_count, own, left, right, far_left, far_right, turned, table, win):
    left_count, right_count = entry(left[META, :], 0), entry(right[META, :], 0)
    table[0:16, :] = own[META, :]
    table[16:32, :] = left[META, :]
    table[32:48, :] = right[META, :]
    table[48:56, :] = far_left[FAR * ROWS :, :]
    table[56:64, :] = far_right[FAR * ROWS :, :]

    def place(source, lane, count):
        spot = pl.ds(pl.multiple_of((lane + MARGIN) * ROWS, 8), count * ROWS)
        win[spot, :] = source[: count * ROWS, :]

    place(far_left, ORIGIN - left_count - FAR, FAR)
    place(left, ORIGIN - left_count, HELD)
    place(own, ORIGIN, HELD)
    place(right, ORIGIN + old_count[0], HELD)
    place(far_right, ORIGIN + old_count[0] + right_count, FAR)
    minor = lax.broadcasted_iota(jnp.int32, (8, LANES), 0)
    root = jnp.sqrt((2 * minor + 1).astype(jnp.float32))

    @pl.loop(0, 2)
    def _(lev):
        for field in range(5):
            for part in range(4):
                block = win[pl.ds(MARGIN * ROWS + field * 8 + part * 2 + lev, LANES, stride=ROWS), :].T
                for z in (2 * part, 2 * part + 1):
                    for x in range(8):
                        at = (z - 2 * part) * 64 + x * 8
                        value = block[at : at + 8, :] * root * (SCALE[z] * SCALE[x])
                        if field == 2:
                            turned[field, lev, pl.ds(z * 64 + x, 8, stride=8), :] = value
                        else:
                            turned[field, lev, pl.ds(z * 64 + x * 8, 8), :] = value


def gather(old_count, own, left, right, far_left, far_right):
    smem = pl.BlockSpec(memory_space=pltpu.SMEM)
    vmem = pl.BlockSpec(memory_space=pltpu.VMEM)
    return pl.pallas_call(
        assemble,
        grid=(1,),
        out_shape=(
            jax.ShapeDtypeStruct((5, 2, 512, LANES), jnp.float32),
            jax.ShapeDtypeStruct((64, LANES), jnp.float32),
        ),
        in_specs=[smem] + [vmem] * 5,
        out_specs=(vmem, vmem),
        scratch_shapes=[
            pltpu.VMEM(((MARGIN + LANES) * ROWS, LANES), jnp.float32),
        ],
        compiler_params=pltpu.CompilerParams(vmem_limit_bytes=14 * 1024 * 1024),
        cost_estimate=pl.CostEstimate(flops=1000000, bytes_accessed=6000000, transcendentals=0),
        name="gather",
    )(old_count, own, left, right, far_left, far_right)


def body(
    place,
    new_count,
    shared,
    table,
    state,
    out,
    start,
    first,
    rise,
    fall,
    lift,
    side,
    rows,
    sem,
):
    row = lax.broadcasted_iota(jnp.int32, shared.shape, 0)
    earlier = jnp.sum(jnp.where(row < place[0] >> 1, shared[...], 0), axis=0)
    column = lax.broadcasted_iota(jnp.int32, (1, 2), 1)
    second = jnp.bitwise_and(place[0], 1)
    left_old = entry(table[16:32, :], 0)
    left_new, right_new = entry(table[16:32, :], 1), entry(table[32:48, :], 1)
    old_begin = jnp.sum(jnp.where(column == 0, earlier, 0)) + second * left_old
    new_begin = jnp.sum(jnp.where(column == 1, earlier, 0)) + second * left_new
    own_new = new_count[0]
    reach = new_begin - old_begin + ORIGIN
    after = reach + own_new
    before = reach - left_new
    lane = lax.broadcasted_iota(jnp.int32, (16, LANES), 1)
    row_lane = lax.broadcasted_iota(jnp.int32, (1, LANES), 1)

    def turn(values, amount):
        return pltpu.roll(values, jnp.bitwise_and(amount, LANES - 1), 1)

    window = jnp.where(
        lane < reach,
        turn(table[16:32, :], before),
        jnp.where(lane < after, turn(table[0:16, :], reach), turn(table[32:48, :], after)),
    )
    window = window.astype(jnp.int32)
    order = window[8:16, :][0:1, :]
    far_before = turn(table[48:56, :], before - 16)[0:1, :].astype(jnp.int32)
    far_after = turn(table[56:64, :], after + right_new)[0:1, :].astype(jnp.int32)
    order = jnp.where(row_lane < before, far_before, order)
    order = jnp.where(row_lane >= after + right_new, far_after, order)
    order = jnp.broadcast_to(order, (8, LANES))
    minor = lax.broadcasted_iota(jnp.int32, (8, LANES), 0)
    lane8 = lax.broadcasted_iota(jnp.int32, (8, LANES), 1)
    masks = [(jnp.maximum(minor, n) <= order).astype(jnp.float32) for n in range(8)]
    lanes, sources, signs = [], [], []
    for face in range(4):
        target = jnp.broadcast_to(window[face : face + 1, :], (8, LANES))
        code = jnp.broadcast_to(window[4 + face : 5 + face, :], (8, LANES))
        wall = target < 0
        lanes.append(jnp.bitwise_and(jnp.where(wall, lane8, target - old_begin + ORIGIN), LANES - 1))
        sources.append(jnp.where(wall, face, code >> 1))
        odd = jnp.bitwise_and(code, 1) * jnp.bitwise_and(minor, 1)
        signs.append(jnp.where(wall, 1.0, 1.0 - 2.0 * odd.astype(jnp.float32)))

    @pl.loop(0, 2)
    def _(lev):
        for field in range(5):
            for z in range(8):
                for x in range(8):
                    spot = pl.ds(z * 64 + x * 8, 8)
                    start[field, lev, spot, :] = state[field, lev, spot, :] * masks[max(z, x)]

    section(start, None, first, rise, fall, lift, side, masks, lanes, sources, signs, False)
    section(first, start, start, rise, fall, lift, side, masks, lanes, sources, signs, True)
    valid = jnp.logical_and(lane8 >= reach, lane8 < after)
    root = jnp.sqrt((2 * minor + 1).astype(jnp.float32))
    shrink = jnp.where(valid, 1.0 / root, 0.0)

    @pl.loop(0, 2)
    def _(lev):
        for field in range(5):
            for part in range(4):
                pieces = []
                for z in (2 * part, 2 * part + 1):
                    for x in range(8):
                        if field == 2:
                            value = start[field, lev, pl.ds(z * 64 + x, 8, stride=8), :]
                        else:
                            value = start[field, lev, pl.ds(z * 64 + x * 8, 8), :]
                        value = value * shrink * (1.0 / (SCALE[z] * SCALE[x]))
                        pieces.append(jnp.where(valid, value, 0.0))
                block = jnp.concatenate(pieces, axis=0).T
                kept = pl.ds(field * 8 + part * 2 + lev, KEPT, stride=ROWS)
                rows[kept, :] = block[32 : 32 + KEPT, :]

    first_row = pl.multiple_of((reach - 32) * ROWS, 8)
    copy = pltpu.make_async_copy(rows.at[pl.ds(first_row, CAP * ROWS)], out, sem)
    copy.start()
    copy.wait()


def advance(place, new_count, shared, table, state):
    smem = pl.BlockSpec(memory_space=pltpu.SMEM)
    vmem = pl.BlockSpec(memory_space=pltpu.VMEM)
    hbm = pl.BlockSpec(memory_space=pl.ANY)
    return pl.pallas_call(
        body,
        out_shape=jax.ShapeDtypeStruct((CAP * ROWS, LANES), jnp.float32),
        in_specs=[smem] * 2 + [vmem] * 3,
        out_specs=hbm,
        scratch_shapes=[
            pltpu.VMEM((5, 2, 512, LANES), jnp.float32),
            pltpu.VMEM((5, 2, 512, LANES), jnp.float32),
            pltpu.VMEM((4, 2, 64, LANES), jnp.float32),
            pltpu.VMEM((4, 2, 64, LANES), jnp.float32),
            pltpu.VMEM((2, 2, 64, LANES), jnp.float32),
            pltpu.VMEM((512, LANES), jnp.float32),
            pltpu.VMEM((KEPT * ROWS, LANES), jnp.float32),
            pltpu.SemaphoreType.DMA,
        ],
        compiler_params=pltpu.CompilerParams(vmem_limit_bytes=16 * 1024 * 1024),
        name="advance",
    )(
        place,
        new_count,
        shared,
        table,
        state,
    )


def local(old_state, old_count, new_count, column_order, neighbour, face_code):
    axes = ("grp", "dev")
    groups, members = lax.axis_size("grp"), lax.axis_size("dev")
    shards = groups * members
    here = lax.axis_index("grp") * members + lax.axis_index("dev")
    place = jnp.reshape(here, (1,)).astype(jnp.int32)

    def along(values, hop):
        return lax.ppermute(values, axes, [(i, (i + hop) % shards) for i in range(shards)])

    own = old_state.reshape(CAP, 5, 2, 4, LANES).transpose(0, 1, 3, 2, 4).reshape(CAP * ROWS, LANES)
    counts = jnp.concatenate([old_count, new_count])
    sibling = lax.ppermute(counts, axes, [(i, i ^ 1) for i in range(shards)])
    geometry = jnp.concatenate([neighbour, face_code, column_order[None, :]], axis=0)
    geometry = jnp.pad(geometry, ((0, 7), (0, LANES - CAP)))
    near, head, tail = pack(old_count, new_count, sibling, geometry, own)
    shared = jnp.broadcast_to((counts + sibling)[None, None, :], (shards // 2, 1, 2))
    near_left, near_right = along(near, 1), along(near, -1)
    far_left, far_right = along(tail, 2), along(head, -2)
    cores = [[2 * pair + core for pair in range(shards // 2)] for core in range(2)]
    shared = lax.all_to_all(shared, axes, 0, 0, axis_index_groups=cores, tiled=True)
    state, table = gather(old_count, near, near_left, near_right, far_left, far_right)
    out = advance(place, new_count, shared, table, state)
    out = out.reshape(CAP, 5, 4, 2, LANES).transpose(0, 1, 3, 2, 4)
    return out.reshape(CAP, 5, 2, 512)


def solution(mesh):
    in_specs = (
        P(("grp", "dev"), None, None, None),
        P(("grp", "dev")),
        P(("grp", "dev")),
        P(("grp", "dev")),
        P(None, ("grp", "dev")),
        P(None, ("grp", "dev")),
    )
    out_specs = P(("grp", "dev"), None, None, None)
    return jax.shard_map(local, mesh=mesh, in_specs=in_specs, out_specs=out_specs, check_vma=False)
```
